512 devices in a mesh: dp: 32 (over z_hi, x, y), code: 16 (over z_lo, core).
Axes of the slice: x: 4, y: 4, z: 16 (z_hi: 2, z_lo: 8; z = z_hi * 8 + z_lo), core: 2. Of those that a mesh axis runs over, the one named last changes fastest.
Arguments:
- latents: bfloat16 [524288, 256], P(('dp', 'code')), may hold values from -6 to 6
- batch_order: int32 [512, 1024], P(('dp', 'code')), may hold values from 0 to 1023, each once within a row
- code_block: int32 [524288, 1], P(('dp', 'code')), may hold values from 0 to 511; in each aligned block of 512 rows (0 to 511, 512 to 1023, ...) at most 2 rows name the same one
- code_offset: int32 [524288], P(('dp', 'code')), may hold values from 0 to 255
- ema_counts: float32 [131072], P(('dp', 'code')), may hold values from 0.5 to 8
- ema_sums: float32 [131072, 256], P(('dp', 'code')), may hold values from -6 to 6
- queries: bfloat16 [32768, 256], P('dp'), may hold values from -6 to 6
Outputs:
- codebook: float32 [131072, 256], P(('dp', 'code'))
- new_counts: float32 [131072], P(('dp', 'code'))
- new_sums: float32 [131072, 256], P(('dp', 'code'))
- nearest: float32 [32768], P('dp')
The draws below stay inside these ranges and needn't reach their ends.
Inputs may be any that keep to these rules, and one draw needn't show every extreme that they name: `code_block`: in each aligned block of 512 rows (one device's batch of one step) no code block is named more than 2 times, and in every draw some block names one code block exactly 2 times. Each row of batch_order names every number of 0 to 1023 once.
All inputs are finite; a program needn't handle non-finite values.
Results may differ from the reference program's by a relative error of at most 0.0009.
Values may be sent and summed in bfloat16 or wider, within the bound.
No kernel may reach another device: no remote copies, remote signals or barrier semaphores. Data moves between devices by JAX's collectives and lax.ppermute only.
A program may use at most 64 MiB of HBM per device.

```python
import math
import jax
import jax.numpy as jnp
import numpy as np
from jax import lax

E = 256
CPD = 256
STEPS = 2
TOK_DEV = 512
CODES = 131072
CAP = 2
ROWS = 524288
QUERIES = 32768
N_DP = 32
N_CODE = 16
DEVICES = 512


def with_ends(values, stream_key, least, top_value):
    shape = values.shape
    spot = [jax.random.randint(jax.random.fold_in(stream_key, axis), (), 0, shape[axis]) for axis in range(len(shape))]
    values = values.at[tuple(spot)].set(least)
    longest = shape.index(max(shape))
    spot[longest] = (spot[longest] + 1) % shape[longest]
    return values.at[tuple(spot)].set(top_value)


def shard_levels(rng, shape, cuts, smallest, top_value):
    def one(axis_at, blocks):
        heights = jax.random.uniform(jax.random.fold_in(jax.random.fold_in(rng, 6), axis_at), (blocks,), jnp.float32, smallest / len(cuts), top_value / len(cuts))
        return jnp.repeat(jnp.exp(heights), shape[axis_at] // blocks).reshape((-1,) + (1,) * (len(shape) - axis_at - 1))

    gain = one(*cuts[0])
    for cut in cuts[1:]:
        gain = gain * one(*cut)
    return gain


def rank_bounds(count, slope):
    loads = [(1 << 20) // math.isqrt(grade ** slope) + 1 for grade in range(1, count + 1)]
    spread = 1 + sum(loads) // (1 << 30)
    return np.cumsum(np.array([max(1, weight // spread) for weight in loads]))


def ranked(stream_key, dims, amount, lean):
    grid = rank_bounds(amount, lean)
    ticket = jax.random.randint(jax.random.fold_in(stream_key, 1), dims, 0, int(grid[amount - 1]))
    rank = jnp.searchsorted(jnp.asarray(grid, jnp.int32), ticket, side="right")
    return jax.random.permutation(jax.random.fold_in(stream_key, 2), amount)[rank].astype(jnp.int32)


def deal_out(own_key, own, number, rows, amount, top, limit, lean):
    ranking = jax.random.permutation(own_key, amount)
    heavy_load, usual = portions_of(amount, rows * top, limit, lean, True), portions_of(amount, rows * top, limit, lean, False)
    places = jnp.arange(amount)

    def named(tallies, rotation):
        used = int((tallies > 0).sum())
        fixed = max(1, used // 4)
        moved = fixed + (places - fixed + rotation * (used - fixed)) % max(1, amount - fixed)
        return jnp.zeros((amount,), jnp.int32).at[ranking[jnp.where(places < fixed, places, moved)]].set(jnp.asarray(tallies, jnp.int32))

    tallies = jnp.where(number % 4 == 0, named(heavy_load, number // 4), named(usual, number - number // 4 - 1))
    mixed = jax.random.permutation(jax.random.fold_in(own, 3), amount)
    donor, receiver = mixed[0:amount // 2 * 2:2], mixed[1:amount // 2 * 2:2]
    margin = jnp.minimum(tallies[donor] - 1, limit - tallies[receiver]) // 2
    margin = jnp.where((donor == ranking[0]) | (receiver == ranking[0]) | (tallies[receiver] == 0), 0, jnp.maximum(margin, 0))
    moved = jax.random.randint(jax.random.fold_in(own, 4), (amount // 2,), 0, 1 << 20) % (margin + 1)
    tallies = tallies.at[donor].add(-moved).at[receiver].add(moved)
    labels = jnp.searchsorted(jnp.cumsum(tallies), jnp.arange(rows * top), side="right").astype(jnp.int32)
    table = labels.reshape(top, rows).T
    table = table[jax.random.permutation(jax.random.fold_in(own, 1), rows)]
    rotation = jax.random.randint(jax.random.fold_in(own, 2), (rows, 1), 0, top)
    return jnp.take_along_axis(table, (jnp.arange(top)[None, :] + rotation) % top, axis=1)


def portions_of(count, total, bound, lean, full):
    portions = [(1 << 20) // math.isqrt(rank ** lean) + 1 for rank in range(1, count + 1)]
    largest = bound if full else min(bound, max(-(-total // count), total * portions[0] // sum(portions)))
    least = 1 if total - largest >= count - 1 else 0
    holding, surplus = [largest] + [least] * (count - 1), total - largest - least * (count - 1)
    while surplus > 0:
        free = [i for i in range(1, count) if holding[i] < largest] or [i for i in range(1, count) if holding[i] < bound]
        whole, remaining = sum([portions[i] for i in free]), surplus
        for i in free:
            addition = min(bound - holding[i], max(1, remaining * portions[i] // whole), surplus)
            holding[i] = holding[i] + addition
            surplus = surplus - addition
    return np.array(holding)


def centred(key, shape, deviation, bound, pieces=(), held_as=jnp.bfloat16):
    values = deviation * jax.random.normal(key, shape, jnp.float32)
    if pieces:
        values = values * shard_levels(key, shape, pieces, -0.22, 0.18)
    return jnp.clip(values, -bound, bound).astype(held_as)


def setup_inputs(seed: int = 0) -> dict:
    seeds = jax.random.split(jax.random.key(seed), 8)
    latents = centred(seeds[0], (ROWS, E), 1.0, 6.0, ((0, 512),))
    batch_order = jax.vmap(lambda own: jax.random.permutation(own, STEPS * TOK_DEV))(jax.random.split(seeds[1], DEVICES)).reshape((DEVICES, STEPS * TOK_DEV)).astype(jnp.int32)
    code_block_keys = jax.random.split(jax.random.fold_in(seeds[2], 1), ROWS // TOK_DEV)
    code_block_turns = jax.random.permutation(jax.random.fold_in(seeds[2], 3), ROWS // TOK_DEV)
    code_block = jax.vmap(lambda own, number: deal_out(jax.random.fold_in(seeds[2], 2), own, number, TOK_DEV, DEVICES, 1, CAP, 3))(code_block_keys, code_block_turns).reshape((ROWS, 1))
    code_offset = with_ends(ranked(seeds[3], (ROWS,), CPD, 2), jax.random.fold_in(seeds[3], 3), 0, CPD - 1).astype(jnp.int32)
    ema_counts = jnp.clip(jnp.exp(math.log(8.0) - 2.7725887 * jax.random.uniform(seeds[4], (CODES,), jnp.float32) ** shard_levels(seeds[4], (CODES,), ((0, 512),), -0.2, 0.2)), 0.5, 8.0)
    ema_sums = centred(seeds[5], (CODES, E), 1.0, 6.0, ((0, 512),), jnp.float32)
    queries = centred(seeds[6], (QUERIES, E), 1.0, 6.0, ((0, 32),))
    return {"latents": latents, "batch_order": batch_order, "code_block": code_block, "code_offset": code_offset, "ema_counts": ema_counts, "ema_sums": ema_sums, "queries": queries}


ema_decay = 0.9


def closest_codes(query_rows, code_rows):
    total_rows = query_rows.shape[0]
    block_rows = math.gcd(total_rows, 512)
    code_norms = jnp.sum(jnp.square(code_rows.astype(jnp.float32)), axis=1)

    def block_minimum(query_block):
        products = jnp.dot(query_block, code_rows.T, preferred_element_type=jnp.float32)
        own_norms = jnp.sum(jnp.square(query_block.astype(jnp.float32)), axis=1)
        distance = (own_norms[:, None] + code_norms[None, :] - 2.0 * products) / E
        return jnp.min(distance, axis=1)

    blocks = query_rows.reshape(total_rows // block_rows, block_rows, E)
    return lax.map(block_minimum, blocks).reshape(total_rows)


def reference(latents, batch_order, code_block, code_offset, ema_counts, ema_sums, queries):
    devices = N_DP * N_CODE
    per_device = STEPS * TOK_DEV
    device_rows = latents.reshape(devices, per_device, E)
    batched = jnp.take_along_axis(device_rows, batch_order[:, :, None], axis=1)
    batched = batched.reshape(devices, STEPS, TOK_DEV, E).astype(jnp.float32)
    code_ids = (code_block.reshape(-1) * CPD + code_offset.reshape(-1)).astype(jnp.int32)
    code_ids = code_ids.reshape(devices, STEPS, TOK_DEV)
    counts_now = ema_counts
    sums_now = ema_sums
    for step_index in range(STEPS):
        step_ids = code_ids[:, step_index].reshape(-1)
        step_rows = batched[:, step_index].reshape(-1, E)
        step_sums = jax.ops.segment_sum(step_rows, step_ids, num_segments=CODES)
        step_counts = jax.ops.segment_sum(jnp.ones(step_ids.shape, jnp.float32), step_ids, num_segments=CODES)
        counts_now = ema_decay * counts_now + (1.0 - ema_decay) * step_counts
        sums_now = ema_decay * sums_now + (1.0 - ema_decay) * step_sums
    codebook = sums_now / counts_now[:, None]
    rounded = codebook.astype(jnp.bfloat16)
    nearest = closest_codes(queries, rounded)
    return (codebook, counts_now, sums_now, nearest)
```

```python
import jax
import jax.numpy as jnp
from jax import lax
from jax.experimental import pallas as pl
from jax.experimental.pallas import tpu as pltpu
from jax.sharding import Mesh, PartitionSpec as P

E = 256
CPD = 256
STEPS = 2
CAP = 2
SLOTS = STEPS * CAP
ema_decay = 0.9

AXES = ("zh", "x", "y", "zl", "core")
SIZES = (2, 4, 4, 8, 2)
PARTNERS = ("x", "y", "core", "zh", "zl")
NT = (((1,), (1,)), ((), ()))

f32 = jnp.float32
bf16 = jnp.bfloat16
i32 = jnp.int32


def iota(shape, dim):
    return lax.broadcasted_iota(i32, shape, dim)


def one_hot(hit):
    return jnp.where(hit, 1.0, 0.0).astype(bf16)


def build_kernel(latents_ref, order_ref, block_ref, offset_ref, rows_ref, table_ref):
    tokens = latents_ref.shape[0]
    step = tokens // STEPS
    block = block_ref[...]
    earlier = one_hot(iota((step, step), 0) < iota((step, step), 1))
    ranks = []
    for t in range(STEPS):
        own = iota((512, step), 0) == block[:, t * step : (t + 1) * step]
        counts = jnp.dot(one_hot(own), earlier, preferred_element_type=f32)
        ranks.append(jnp.sum(jnp.where(own, counts, 0.0), axis=0, keepdims=True))
    rank = jnp.concatenate(ranks, axis=1).astype(i32)
    position = iota((1, tokens), 1)
    slot = jnp.where(position >= step, CAP, 0) + rank
    z_row = ((block >> 8) << 3) | ((block >> 1) & 7)
    plane = (((block >> 4) & 15) << 1) | (block & 1)
    place = (plane * 16 + z_row) * SLOTS + slot
    code = (offset_ref[...] + 1).astype(f32)
    rows_hit = jnp.where(iota((16, tokens), 0) == z_row, code, 0.0).astype(bf16)
    lanes_hit = one_hot(iota((128, tokens), 0) == plane * SLOTS + slot)
    table_ref[...] = lax.dot_general(rows_hit, lanes_hit, NT, preferred_element_type=f32)
    digits = jnp.where(iota((8, tokens), 0) == 0, place >> 6, place & 63).astype(f32).astype(bf16)
    stored = one_hot(iota((tokens, tokens), 0) == order_ref[...])
    pair = lax.dot_general(digits, stored, NT, preferred_element_type=f32).astype(i32)
    place = pair[0:1] * 64 + pair[1:2]
    latents = latents_ref[...]
    chunk = 512
    low = iota((chunk // 8, 8, 128), 1) < 4
    for c in range(512 * SLOTS // chunk):
        pick = one_hot(iota((chunk, tokens), 0) + c * chunk == place)
        got = jnp.dot(pick, latents, preferred_element_type=f32)
        a = got[:, :128].reshape(chunk // 8, 8, 128)
        b = got[:, 128:].reshape(chunk // 8, 8, 128)
        first = jnp.where(low, a, pltpu.roll(b, 4, 1))
        second = jnp.where(low, pltpu.roll(a, 4, 1), b)
        both = jnp.stack([first, second], axis=1).reshape(chunk // 4, 8, 128)
        rows_ref[c * (chunk // 4) : (c + 1) * (chunk // 4)] = both.astype(bf16)


def build(latents, order, block, offset):
    return pl.pallas_call(
        build_kernel,
        out_shape=(
            jax.ShapeDtypeStruct((512, 8, 128), bf16),
            jax.ShapeDtypeStruct((16, 128), f32),
        ),
        compiler_params=pltpu.CompilerParams(vmem_limit_bytes=48 << 20),
        cost_estimate=pl.CostEstimate(flops=3 << 30, bytes_accessed=2 << 20, transcendentals=0),
        name="build",
    )(latents, order, block, offset)


def update_kernel(mine_ref, rows_ref, table_ref, count_col_ref, count_row_ref, sums_ref,
                  codebook_ref, counts_ref, new_sums_ref, rounded_ref, hit_ref):
    mine = mine_ref[0]
    lane = iota((512, 128), 1)
    table = jnp.where((lane >> 2) == mine, table_ref[...], 0.0).astype(bf16)
    spread = one_hot((iota((128, 128), 0) & 3) == (iota((128, 128), 1) & 3))
    spread = jnp.dot(table, spread, preferred_element_type=f32)
    keep = (iota((512, 128), 0) & 31) == (lane >> 2)
    code = jnp.sum(jnp.where(keep, spread, 0.0).reshape(16, 32, 128), axis=1).astype(i32)
    local = iota((2 * CPD, 128), 0)
    step = ((iota((2 * CPD, 128), 1) & 3) >> 1) == (local >> 8)
    local = jnp.where(step, (local & 255) + 1, -1)
    for i in range(16):
        hit_ref[:, i * 128 : (i + 1) * 128] = one_hot(local == code[i : i + 1])
    pairs = rows_ref[...].astype(f32).reshape(256, 2, 8, 128)
    first, second = pairs[:, 0], pairs[:, 1]
    low = iota((256, 8, 128), 1) < 4
    left = jnp.where(low, first, pltpu.roll(second, 4, 1)).reshape(2048, 128)
    right = jnp.where(low, pltpu.roll(first, 4, 1), second).reshape(2048, 128)
    hits = hit_ref[...]
    sums_left = jnp.dot(hits, left.astype(bf16), preferred_element_type=f32)
    sums_right = jnp.dot(hits, right.astype(bf16), preferred_element_type=f32)
    step_sums = jnp.concatenate([sums_left, sums_right], axis=1)
    step_cols = jnp.dot(hits, jnp.ones((2048, 128), bf16), preferred_element_type=f32)
    step_rows = lax.dot_general(jnp.ones((8, 2048), bf16), hits, NT, preferred_element_type=f32)
    sums = sums_ref[...]
    cols = count_col_ref[...]
    rows = count_row_ref[...]
    for t in range(STEPS):
        part = slice(t * CPD, (t + 1) * CPD)
        sums = ema_decay * sums + (1.0 - ema_decay) * step_sums[part]
        cols = ema_decay * cols + (1.0 - ema_decay) * step_cols[part, 0:1]
        rows = ema_decay * rows + (1.0 - ema_decay) * step_rows[0:1, part]
    book = sums / cols
    codebook_ref[...] = book
    rounded_ref[...] = book.astype(bf16)
    new_sums_ref[...] = sums
    counts_ref[...] = rows


def update(mine, rows, table, counts, sums):
    vmem = pl.BlockSpec(memory_space=pltpu.VMEM)
    return pl.pallas_call(
        update_kernel,
        out_shape=(
            jax.ShapeDtypeStruct((CPD, E), f32),
            jax.ShapeDtypeStruct((1, CPD), f32),
            jax.ShapeDtypeStruct((CPD, E), f32),
            jax.ShapeDtypeStruct((CPD, E), bf16),
        ),
        in_specs=[pl.BlockSpec(memory_space=pltpu.SMEM)] + [vmem] * 5,
        out_specs=(vmem,) * 4,
        scratch_shapes=[pltpu.VMEM((2 * CPD, 2048), bf16)],
        compiler_params=pltpu.CompilerParams(vmem_limit_bytes=48 << 20),
        cost_estimate=pl.CostEstimate(flops=1 << 30, bytes_accessed=3 << 20, transcendentals=0),
        name="update",
    )(mine, rows, table, counts.reshape(CPD, 1), counts.reshape(1, CPD), sums)


def nearest_kernel(codes_ref, queries_ref, out_ref, best_ref):
    groups, width = out_ref.shape
    tile = 256
    for c in range(codes_ref.shape[0] // tile):
        codes = codes_ref[c * tile : (c + 1) * tile].astype(f32)
        norms = jnp.sum(codes * codes, axis=1, keepdims=True)
        scaled = (-2.0 * codes).astype(bf16)
        for g in range(groups):
            part = queries_ref[g * width : (g + 1) * width]
            value = lax.dot_general(scaled, part, NT, preferred_element_type=f32) + norms
            value = jnp.min(value.reshape(tile // 8, 8, width), axis=0)
            best_ref[g] = value if c == 0 else jnp.minimum(best_ref[g], value)
    for g in range(groups):
        out_ref[g : g + 1] = jnp.min(best_ref[g], axis=0, keepdims=True)


def nearest_codes(codes, queries):
    return pl.pallas_call(
        nearest_kernel,
        out_shape=jax.ShapeDtypeStruct((8, 512), f32),
        scratch_shapes=[pltpu.VMEM((8, 8, 512), f32)],
        compiler_params=pltpu.CompilerParams(vmem_limit_bytes=48 << 20),
        cost_estimate=pl.CostEstimate(flops=5 << 30, bytes_accessed=3 << 20, transcendentals=0),
        name="nearest",
    )(codes, queries)


def gather_queries(queries):
    share = queries.shape[0] // 8
    slice_ = lax.dynamic_slice_in_dim(queries, lax.axis_index("zl") * share, share, 0)
    both = lax.all_gather(slice_, ("zh", "zl"), axis=0, tiled=True)
    half = queries.shape[0] // 2
    both = both.reshape(2, 2 * half, E)
    mine = lax.dynamic_slice_in_dim(both, lax.axis_index("core") * half, half, 1)
    return lax.all_gather(mine.reshape(2 * half, E), "y", axis=0, tiled=True)


def body(latents, batch_order, code_block, code_offset, ema_counts, ema_sums, queries):
    batch_queries = gather_queries(queries)
    own = jnp.sum(jnp.square(queries.astype(f32)), axis=1)
    rows, table = build(
        latents, batch_order, code_block.reshape(1, -1), code_offset.reshape(1, -1)
    )
    got = lax.all_to_all(rows, PARTNERS, 0, 0, tiled=True)
    z_table = lax.all_to_all(table, ("zh", "zl"), 0, 0, tiled=True)
    tables = lax.all_gather(z_table, ("x", "y", "core"), axis=0, tiled=True)
    mine = lax.axis_index(("x", "y", "core")).astype(i32).reshape(1)
    codebook, counts, sums, rounded = update(mine, got, tables, ema_counts, ema_sums)
    codes = lax.all_gather(rounded, "x", axis=0, tiled=True)
    other = lax.ppermute(codes, "core", [(0, 1), (1, 0)])
    codes = jnp.concatenate([codes, other], axis=0)
    best = nearest_codes(codes, batch_queries)
    sent = jnp.broadcast_to(best[:, None, :], (8, 8, 512)).reshape(64, 4, 128)
    found = jnp.min(lax.all_to_all(sent, ("y", "zh", "zl"), 0, 0, tiled=True), axis=0)
    found = lax.all_gather(found, "core", axis=0, tiled=True).reshape(-1)
    nearest = (own + found) / E
    return (codebook, counts.reshape(-1), sums, nearest)


def solution(mesh):
    fine = Mesh(mesh.devices.reshape(SIZES), AXES)
    placed = (
        P(AXES, None),
        P(AXES, None),
        P(AXES, None),
        P(AXES),
        P(AXES),
        P(AXES, None),
        P(("zh", "x", "y"), None),
    )
    return jax.shard_map(
        body,
        mesh=fine,
        in_specs=placed,
        out_specs=(P(AXES, None), P(AXES), P(AXES, None), P(("zh", "x", "y"))),
        check_vma=False,
    )
```

```python
import jax
import jax.numpy as jnp
from jax import lax
from jax.experimental import pallas as pl
from jax.experimental.pallas import tpu as pltpu
from jax.sharding import Mesh, PartitionSpec as P

E = 256
CPD = 256
STEPS = 2
CAP = 2
SLOTS = STEPS * CAP
ema_decay = 0.9

AXES = ("zh", "x", "y", "zl", "core")
SIZES = (2, 4, 4, 8, 2)
PARTNERS = ("x", "y", "core", "zh", "zl")
NT = (((1,), (1,)), ((), ()))

f32 = jnp.float32
bf16 = jnp.bfloat16
i32 = jnp.int32


def iota(shape, dim):
    return lax.broadcasted_iota(i32, shape, dim)


def one_hot(hit):
    return jnp.where(hit, 1.0, 0.0).astype(bf16)


def build_kernel(latents_hbm, order_hbm, block_hbm, offset_hbm, rows_ref, table_ref,
                 latents_ref, order_ref, block_ref, offset_ref, sems):
    tokens = latents_ref.shape[0]
    step = tokens // STEPS
    copies = [
        pltpu.make_async_copy(block_hbm, block_ref, sems.at[0]),
        pltpu.make_async_copy(offset_hbm, offset_ref, sems.at[1]),
        pltpu.make_async_copy(order_hbm, order_ref, sems.at[2]),
        pltpu.make_async_copy(latents_hbm, latents_ref, sems.at[3]),
    ]
    for copy in copies:
        copy.start()
    copies[0].wait()
    block = block_ref[...]
    earlier = one_hot(iota((step, step), 0) < iota((step, step), 1))
    ranks = []
    for t in range(STEPS):
        own = iota((512, step), 0) == block[:, t * step : (t + 1) * step]
        counts = jnp.dot(one_hot(own), earlier, preferred_element_type=f32)
        ranks.append(jnp.sum(jnp.where(own, counts, 0.0), axis=0, keepdims=True))
    rank = jnp.concatenate(ranks, axis=1).astype(i32)
    position = iota((1, tokens), 1)
    slot = jnp.where(position >= step, CAP, 0) + rank
    z_row = ((block >> 8) << 3) | ((block >> 1) & 7)
    plane = (((block >> 4) & 15) << 1) | (block & 1)
    place = (plane * 16 + z_row) * SLOTS + slot
    copies[1].wait()
    code = (offset_ref[...] + 1).astype(f32)
    rows_hit = jnp.where(iota((16, tokens), 0) == z_row, code, 0.0).astype(bf16)
    lanes_hit = one_hot(iota((128, tokens), 0) == plane * SLOTS + slot)
    table_ref[...] = lax.dot_general(rows_hit, lanes_hit, NT, preferred_element_type=f32)
    digits = jnp.where(iota((8, tokens), 0) == 0, place >> 6, place & 63).astype(f32).astype(bf16)
    copies[2].wait()
    stored = one_hot(iota((tokens, tokens), 0) == order_ref[...])
    pair = lax.dot_general(digits, stored, NT, preferred_element_type=f32).astype(i32)
    place = pair[0:1] * 64 + pair[1:2]
    copies[3].wait()
    latents = latents_ref[...]
    chunk = 512
    low = iota((chunk // 8, 8, 128), 1) < 4
    for c in range(512 * SLOTS // chunk):
        pick = one_hot(iota((chunk, tokens), 0) + c * chunk == place)
        got = jnp.dot(pick, latents, preferred_element_type=f32)
        a = got[:, :128].reshape(chunk // 8, 8, 128)
        b = got[:, 128:].reshape(chunk // 8, 8, 128)
        first = jnp.where(low, a, pltpu.roll(b, 4, 1))
        second = jnp.where(low, pltpu.roll(a, 4, 1), b)
        both = jnp.stack([first, second], axis=1).reshape(chunk // 4, 8, 128)
        rows_ref[c * (chunk // 4) : (c + 1) * (chunk // 4)] = both.astype(bf16)


def build(latents, order, block, offset):
    return pl.pallas_call(
        build_kernel,
        out_shape=(
            jax.ShapeDtypeStruct((512, 8, 128), bf16),
            jax.ShapeDtypeStruct((16, 128), f32),
        ),
        in_specs=[pl.BlockSpec(memory_space=pltpu.HBM)] * 4,
        scratch_shapes=[
            pltpu.VMEM((1024, E), bf16),
            pltpu.VMEM((1, 1024), i32),
            pltpu.VMEM((1, 1024), i32),
            pltpu.VMEM((1, 1024), i32),
            pltpu.SemaphoreType.DMA((4,)),
        ],
        compiler_params=pltpu.CompilerParams(vmem_limit_bytes=60 << 20),
        cost_estimate=pl.CostEstimate(flops=3 << 30, bytes_accessed=2 << 20, transcendentals=0),
        name="build",
    )(latents, order, block, offset)


def update_kernel(mine_ref, rows_ref, table_ref, count_col_ref, count_row_ref, sums_ref,
                  codebook_ref, counts_ref, new_sums_ref, rounded_ref, hit_ref):
    mine = mine_ref[0]
    lane = iota((512, 128), 1)
    table = jnp.where((lane >> 2) == mine, table_ref[...], 0.0).astype(bf16)
    spread = one_hot((iota((128, 128), 0) & 3) == (iota((128, 128), 1) & 3))
    spread = jnp.dot(table, spread, preferred_element_type=f32)
    keep = (iota((512, 128), 0) & 31) == (lane >> 2)
    code = jnp.sum(jnp.where(keep, spread, 0.0).reshape(16, 32, 128), axis=1).astype(i32)
    local = iota((2 * CPD, 128), 0)
    step = ((iota((2 * CPD, 128), 1) & 3) >> 1) == (local >> 8)
    local = jnp.where(step, (local & 255) + 1, -1)
    for i in range(16):
        hit_ref[:, i * 128 : (i + 1) * 128] = one_hot(local == code[i : i + 1])
    pairs = rows_ref[...].astype(f32).reshape(256, 2, 8, 128)
    first, second = pairs[:, 0], pairs[:, 1]
    low = iota((256, 8, 128), 1) < 4
    left = jnp.where(low, first, pltpu.roll(second, 4, 1)).reshape(2048, 128)
    right = jnp.where(low, pltpu.roll(first, 4, 1), second).reshape(2048, 128)
    hits = hit_ref[...]
    sums_left = jnp.dot(hits, left.astype(bf16), preferred_element_type=f32)
    sums_right = jnp.dot(hits, right.astype(bf16), preferred_element_type=f32)
    step_sums = jnp.concatenate([sums_left, sums_right], axis=1)
    step_cols = jnp.dot(hits, jnp.ones((2048, 128), bf16), preferred_element_type=f32)
    step_rows = lax.dot_general(jnp.ones((8, 2048), bf16), hits, NT, preferred_element_type=f32)
    sums = sums_ref[...]
    cols = count_col_ref[...]
    rows = count_row_ref[...]
    for t in range(STEPS):
        part = slice(t * CPD, (t + 1) * CPD)
        sums = ema_decay * sums + (1.0 - ema_decay) * step_sums[part]
        cols = ema_decay * cols + (1.0 - ema_decay) * step_cols[part, 0:1]
        rows = ema_decay * rows + (1.0 - ema_decay) * step_rows[0:1, part]
    book = sums / cols
    codebook_ref[...] = book
    rounded_ref[...] = book.astype(bf16)
    new_sums_ref[...] = sums
    counts_ref[...] = rows


def update(mine, rows, table, counts, sums):
    vmem = pl.BlockSpec(memory_space=pltpu.VMEM)
    return pl.pallas_call(
        update_kernel,
        out_shape=(
            jax.ShapeDtypeStruct((CPD, E), f32),
            jax.ShapeDtypeStruct((1, CPD), f32),
            jax.ShapeDtypeStruct((CPD, E), f32),
            jax.ShapeDtypeStruct((CPD, E), bf16),
        ),
        in_specs=[pl.BlockSpec(memory_space=pltpu.SMEM)] + [vmem] * 5,
        out_specs=(vmem,) * 4,
        scratch_shapes=[pltpu.VMEM((2 * CPD, 2048), bf16)],
        compiler_params=pltpu.CompilerParams(vmem_limit_bytes=48 << 20),
        cost_estimate=pl.CostEstimate(flops=1 << 30, bytes_accessed=3 << 20, transcendentals=0),
        name="update",
    )(mine, rows, table, counts.reshape(CPD, 1), counts.reshape(1, CPD), sums)


def nearest_kernel(near_ref, far_ref, queries_ref, out_ref, best_ref):
    groups, _, width = best_ref.shape
    tile = 256
    first = True
    for codes_ref in (near_ref, far_ref):
        for c in range(codes_ref.shape[0] // tile):
            codes = codes_ref[c * tile : (c + 1) * tile].astype(f32)
            norms = jnp.sum(codes * codes, axis=1, keepdims=True)
            scaled = (-2.0 * codes).astype(bf16)
            for g in range(groups):
                part = queries_ref[g * width : (g + 1) * width]
                value = lax.dot_general(scaled, part, NT, preferred_element_type=f32) + norms
                value = jnp.min(value.reshape(tile // 8, 8, width), axis=0)
                best_ref[g] = value if first else jnp.minimum(best_ref[g], value)
            first = False
    for y in range(4):
        lines = []
        for g in (2 * y, 2 * y + 1):
            line = jnp.min(best_ref[g], axis=0, keepdims=True)
            lines += [line[:, j * 128 : (j + 1) * 128] for j in range(4)]
        tile_ = jnp.concatenate(lines, axis=0)
        out_ref[y * 16 : (y + 1) * 16] = jnp.broadcast_to(tile_[None], (16, 8, 128))


def nearest_codes(near, far, queries):
    return pl.pallas_call(
        nearest_kernel,
        out_shape=jax.ShapeDtypeStruct((64, 8, 128), f32),
        scratch_shapes=[pltpu.VMEM((8, 8, 512), f32)],
        compiler_params=pltpu.CompilerParams(vmem_limit_bytes=48 << 20),
        cost_estimate=pl.CostEstimate(flops=5 << 30, bytes_accessed=3 << 20, transcendentals=0),
        name="nearest",
    )(near, far, queries)


def body(latents, batch_order, code_block, code_offset, ema_counts, ema_sums, queries):
    row_queries = lax.all_gather(queries, "y", axis=0, tiled=True)
    own = jnp.sum(jnp.square(queries.astype(f32)), axis=1)
    rows, table = build(
        latents, batch_order, code_block.reshape(1, -1), code_offset.reshape(1, -1)
    )
    got = lax.all_to_all(rows, PARTNERS, 0, 0, tiled=True)
    z_tables = lax.all_gather(table, ("zh", "zl"), axis=0)
    z_table = lax.dynamic_index_in_dim(z_tables, lax.axis_index(("zh", "zl")), 1, keepdims=False)
    tables = lax.all_gather(z_table, ("x", "y", "core"), axis=0, tiled=True)
    mine = lax.axis_index(("x", "y", "core")).astype(i32).reshape(1)
    codebook, counts, sums, rounded = update(mine, got, tables, ema_counts, ema_sums)
    mirrored = lax.ppermute(rounded, ("zh", "zl"), [(z, 15 - z) for z in range(16)])
    near = lax.all_gather(rounded, "x", axis=0, tiled=True)
    far = lax.all_gather(mirrored, "x", axis=0, tiled=True)
    best = nearest_codes(near, far, row_queries)
    found = jnp.min(lax.all_to_all(best, ("y", "zl", "core"), 0, 0, tiled=True), axis=0)
    nearest = (own + found.reshape(-1)) / E
    return (codebook, counts.reshape(-1), sums, nearest)


def solution(mesh):
    fine = Mesh(mesh.devices.reshape(SIZES), AXES)
    placed = (
        P(AXES, None),
        P(AXES, None),
        P(AXES, None),
        P(AXES),
        P(AXES),
        P(AXES, None),
        P(("zh", "x", "y"), None),
    )
    return jax.shard_map(
        body,
        mesh=fine,
        in_specs=placed,
        out_specs=(P(AXES, None), P(AXES), P(AXES, None), P(("zh", "x", "y"))),
        check_vma=False,
    )
```

```python
import jax
import jax.numpy as jnp
from jax import lax
from jax.experimental import pallas as pl
from jax.experimental.pallas import tpu as pltpu
from jax.sharding import Mesh, PartitionSpec as P

E = 256
CPD = 256
STEPS = 2
CAP = 2
SLOTS = STEPS * CAP
ema_decay = 0.9

AXES = ("zh", "x", "y", "zl", "core")
SIZES = (2, 4, 4, 8, 2)
NT = (((1,), (1,)), ((), ()))

f32 = jnp.float32
bf16 = jnp.bfloat16
i32 = jnp.int32


def iota(shape, dim):
    return lax.broadcasted_iota(i32, shape, dim)


def one_hot(hit):
    return jnp.where(hit, 1.0, 0.0).astype(bf16)


def build_kernel(latents_hbm, order_hbm, block_hbm, offset_hbm, rows_ref,
                 latents_ref, order_ref, block_ref, offset_ref, sems):
    tokens = latents_ref.shape[0]
    step = tokens // STEPS
    copies = [
        pltpu.make_async_copy(block_hbm, block_ref, sems.at[0]),
        pltpu.make_async_copy(offset_hbm, offset_ref, sems.at[1]),
        pltpu.make_async_copy(order_hbm, order_ref, sems.at[2]),
        pltpu.make_async_copy(latents_hbm, latents_ref, sems.at[3]),
    ]
    for copy in copies:
        copy.start()
    copies[0].wait()
    block = block_ref[...]
    earlier = one_hot(iota((step, step), 0) < iota((step, step), 1))
    ranks = []
    for t in range(STEPS):
        own = iota((512, step), 0) == block[:, t * step : (t + 1) * step]
        counts = jnp.dot(one_hot(own), earlier, preferred_element_type=f32)
        ranks.append(jnp.sum(jnp.where(own, counts, 0.0), axis=0, keepdims=True))
    rank = jnp.concatenate(ranks, axis=1).astype(i32)
    position = iota((1, tokens), 1)
    slot = jnp.where(position >= step, CAP, 0) + rank
    place = block * SLOTS + slot
    copies[1].wait()
    code = (offset_ref[...] + 1).astype(f32)
    lanes = jnp.where((iota((128, tokens), 0) & 3) == slot, code, 0.0).astype(bf16)
    named = one_hot((iota((1024, tokens), 0) >> 1) == block)
    labels = lax.dot_general(named, lanes, NT, preferred_element_type=f32).reshape(128, 8, 128)
    digits = jnp.where(iota((8, tokens), 0) == 0, place >> 6, place & 63).astype(f32).astype(bf16)
    copies[2].wait()
    stored = one_hot(iota((tokens, tokens), 0) == order_ref[...])
    pair = lax.dot_general(digits, stored, NT, preferred_element_type=f32).astype(i32)
    place = pair[0:1] * 64 + pair[1:2]
    copies[3].wait()
    latents = latents_ref[...]
    chunk = 512
    low = iota((chunk // 8, 8, 128), 1) < 4
    row = iota((chunk // 16, 8, 128), 1)
    for c in range(512 * SLOTS // chunk):
        pick = one_hot(iota((chunk, tokens), 0) + c * chunk == place)
        got = jnp.dot(pick, latents, preferred_element_type=f32)
        a = got[:, :128].reshape(chunk // 8, 8, 128)
        b = got[:, 128:].reshape(chunk // 8, 8, 128)
        first = jnp.where(low, a, pltpu.roll(b, 4, 1))
        second = jnp.where(low, pltpu.roll(a, 4, 1), b)
        m = jnp.stack([first, second], axis=1).reshape(chunk // 16, 4, 8, 128)
        label = labels[c * (chunk // 16) : (c + 1) * (chunk // 16)]
        m1 = pltpu.roll(m[:, 1], 2, 1)
        m2 = pltpu.roll(m[:, 2], 4, 1)
        m3 = pltpu.roll(m[:, 3], 6, 1)
        tiles = [
            m[:, 0],
            jnp.where(row < 2, label, m1),
            jnp.where(row < 2, m1, jnp.where(row < 4, label, m2)),
            jnp.where(row < 4, m2, jnp.where(row < 6, label, m3)),
            jnp.where(row < 6, m3, label),
        ]
        count = chunk // 16 * 40
        rows_ref[c * count : (c + 1) * count] = (
            jnp.stack(tiles, axis=1).reshape(count, 128).astype(bf16)
        )


def build(latents, order, block, offset):
    return pl.pallas_call(
        build_kernel,
        out_shape=jax.ShapeDtypeStruct((512 * 10, 128), bf16),
        in_specs=[pl.BlockSpec(memory_space=pltpu.HBM)] * 4,
        scratch_shapes=[
            pltpu.VMEM((1024, E), bf16),
            pltpu.VMEM((1, 1024), i32),
            pltpu.VMEM((1, 1024), i32),
            pltpu.VMEM((1, 1024), i32),
            pltpu.SemaphoreType.DMA((4,)),
        ],
        compiler_params=pltpu.CompilerParams(vmem_limit_bytes=60 << 20),
        cost_estimate=pl.CostEstimate(flops=3 << 30, bytes_accessed=2 << 20, transcendentals=0),
        name="build",
    )(latents, order, block, offset)


def update_kernel(rows_ref, count_col_ref, count_row_ref, sums_ref,
                  codebook_ref, counts_ref, new_sums_ref, rounded_ref, hit_ref):
    t0, t1, t2, t3, t4 = jnp.split(rows_ref[...].astype(f32).reshape(128, 5, 8, 128), 5, axis=1)
    t0, t1, t2, t3, t4 = t0[:, 0], t1[:, 0], t2[:, 0], t3[:, 0], t4[:, 0]
    row = iota((128, 8, 128), 1)
    label = jnp.where(row < 2, t1, jnp.where(row < 4, t2, jnp.where(row < 6, t3, t4)))
    keep = iota((64, 128), 0) == 2 * (iota((64, 128), 1) >> 2)
    code = jnp.sum(jnp.where(keep, label.reshape(16, 64, 128), 0.0), axis=1).astype(i32)
    local = iota((2 * CPD, 128), 0)
    step = ((iota((2 * CPD, 128), 1) & 3) >> 1) == (local >> 8)
    local = jnp.where(step, (local & 255) + 1, -1)
    for i in range(16):
        hit_ref[:, i * 128 : (i + 1) * 128] = one_hot(local == code[i : i + 1])
    m1 = jnp.where(row < 6, pltpu.roll(t1, 6, 1), pltpu.roll(t2, 6, 1))
    m2 = jnp.where(row < 4, pltpu.roll(t2, 4, 1), pltpu.roll(t3, 4, 1))
    m3 = jnp.where(row < 2, pltpu.roll(t3, 2, 1), pltpu.roll(t4, 2, 1))
    first = jnp.stack([t0, m2], axis=1).reshape(256, 8, 128)
    second = jnp.stack([m1, m3], axis=1).reshape(256, 8, 128)
    low = iota((256, 8, 128), 1) < 4
    left = jnp.where(low, first, pltpu.roll(second, 4, 1)).reshape(2048, 128)
    right = jnp.where(low, pltpu.roll(first, 4, 1), second).reshape(2048, 128)
    hits = hit_ref[...]
    sums_left = jnp.dot(hits, left.astype(bf16), preferred_element_type=f32)
    sums_right = jnp.dot(hits, right.astype(bf16), preferred_element_type=f32)
    step_sums = jnp.concatenate([sums_left, sums_right], axis=1)
    step_cols = jnp.dot(hits, jnp.ones((2048, 128), bf16), preferred_element_type=f32)
    step_rows = lax.dot_general(jnp.ones((8, 2048), bf16), hits, NT, preferred_element_type=f32)
    sums = sums_ref[...]
    cols = count_col_ref[...]
    rows = count_row_ref[...]
    for t in range(STEPS):
        part = slice(t * CPD, (t + 1) * CPD)
        sums = ema_decay * sums + (1.0 - ema_decay) * step_sums[part]
        cols = ema_decay * cols + (1.0 - ema_decay) * step_cols[part, 0:1]
        rows = ema_decay * rows + (1.0 - ema_decay) * step_rows[0:1, part]
    book = sums / cols
    codebook_ref[...] = book
    rounded_ref[...] = book.astype(bf16)
    new_sums_ref[...] = sums
    counts_ref[...] = rows


def update(rows, counts, sums):
    vmem = pl.BlockSpec(memory_space=pltpu.VMEM)
    return pl.pallas_call(
        update_kernel,
        out_shape=(
            jax.ShapeDtypeStruct((CPD, E), f32),
            jax.ShapeDtypeStruct((1, CPD), f32),
            jax.ShapeDtypeStruct((CPD, E), f32),
            jax.ShapeDtypeStruct((CPD, E), bf16),
        ),
        in_specs=[vmem] * 4,
        out_specs=(vmem,) * 4,
        scratch_shapes=[pltpu.VMEM((2 * CPD, 2048), bf16)],
        compiler_params=pltpu.CompilerParams(vmem_limit_bytes=48 << 20),
        cost_estimate=pl.CostEstimate(flops=1 << 30, bytes_accessed=3 << 20, transcendentals=0),
        name="update",
    )(rows, counts.reshape(CPD, 1), counts.reshape(1, CPD), sums)


def nearest_kernel(near_ref, far_ref, queries_ref, out_ref, best_ref):
    groups, _, width = best_ref.shape
    tile = 256
    first = True
    for codes_ref in (near_ref, far_ref):
        for c in range(codes_ref.shape[0] // tile):
            codes = codes_ref[c * tile : (c + 1) * tile].astype(f32)
            norms = jnp.sum(codes * codes, axis=1, keepdims=True)
            scaled = (-2.0 * codes).astype(bf16)
            for g in range(groups):
                part = queries_ref[g * width : (g + 1) * width]
                value = lax.dot_general(scaled, part, NT, preferred_element_type=f32) + norms
                value = jnp.min(value.reshape(tile // 8, 8, width), axis=0)
                best_ref[g] = value if first else jnp.minimum(best_ref[g], value)
            first = False
    for g in range(groups):
        line = jnp.min(best_ref[g], axis=0, keepdims=True)
        part = jnp.concatenate([line[:, j * 128 : (j + 1) * 128] for j in range(4)], axis=0)
        y, core = g // 2, g % 2
        for zl in range(8):
            out_ref[y * 16 + zl * 2 + core] = part


def nearest_codes(near, far, queries):
    return pl.pallas_call(
        nearest_kernel,
        out_shape=jax.ShapeDtypeStruct((64, 4, 128), f32),
        scratch_shapes=[pltpu.VMEM((8, 8, 512), f32)],
        compiler_params=pltpu.CompilerParams(vmem_limit_bytes=48 << 20),
        cost_estimate=pl.CostEstimate(flops=5 << 30, bytes_accessed=3 << 20, transcendentals=0),
        name="nearest",
    )(near, far, queries)


def body(latents, batch_order, code_block, code_offset, ema_counts, ema_sums, queries):
    row_queries = lax.all_gather(queries, "y", axis=0, tiled=True)
    own = jnp.sum(jnp.square(queries.astype(f32)), axis=1)
    rows = build(
        latents, batch_order, code_block.reshape(1, -1), code_offset.reshape(1, -1)
    )
    got = lax.all_to_all(rows.reshape(512, 5, 2, 128), AXES, 0, 0, tiled=True)
    codebook, counts, sums, rounded = update(got.reshape(5120, 128), ema_counts, ema_sums)
    mirrored = lax.ppermute(rounded, ("zh", "zl"), [(z, 15 - z) for z in range(16)])
    near = lax.all_gather(rounded, "x", axis=0, tiled=True)
    far = lax.all_gather(mirrored, "x", axis=0, tiled=True)
    best = nearest_codes(near, far, row_queries)
    found = jnp.min(lax.all_to_all(best, ("y", "zl", "core"), 0, 0, tiled=True), axis=0)
    found = lax.all_gather(found, "core", axis=0, tiled=True).reshape(-1)
    nearest = (own + found) / E
    return (codebook, counts.reshape(-1), sums, nearest)


def solution(mesh):
    fine = Mesh(mesh.devices.reshape(SIZES), AXES)
    placed = (
        P(AXES, None),
        P(AXES, None),
        P(AXES, None),
        P(AXES),
        P(AXES),
        P(AXES, None),
        P(("zh", "x", "y"), None),
    )
    return jax.shard_map(
        body,
        mesh=fine,
        in_specs=placed,
        out_specs=(P(AXES, None), P(AXES), P(AXES, None), P(("zh", "x", "y"))),
        check_vma=False,
    )
```

```python
import functools

import jax
import jax.numpy as jnp
from jax import lax
from jax.experimental import pallas as pl
from jax.experimental.pallas import tpu as pltpu
from jax.sharding import Mesh, PartitionSpec as P

E = 256
CPD = 256
STEPS = 2
CAP = 2
SLOTS = STEPS * CAP
ema_decay = 0.9

AXES = ("zh", "x", "y", "zl", "core")
SIZES = (2, 4, 4, 8, 2)
NT = (((1,), (1,)), ((), ()))

f32 = jnp.float32
bf16 = jnp.bfloat16
i32 = jnp.int32


def iota(shape, dim):
    return lax.broadcasted_iota(i32, shape, dim)


def one_hot(hit):
    return jnp.where(hit, 1.0, 0.0).astype(bf16)


def build_kernel(core_ref, latents_hbm, order_hbm, block_hbm, offset_hbm, rows_ref,
                 latents_ref, order_ref, block_ref, offset_ref, sems):
    tokens = latents_ref.shape[0]
    step = tokens // STEPS
    copies = [
        pltpu.make_async_copy(block_hbm, block_ref, sems.at[0]),
        pltpu.make_async_copy(offset_hbm, offset_ref, sems.at[1]),
        pltpu.make_async_copy(order_hbm, order_ref, sems.at[2]),
        pltpu.make_async_copy(latents_hbm, latents_ref, sems.at[3]),
    ]
    for copy in copies:
        copy.start()
    copies[0].wait()
    block = block_ref[...] ^ core_ref[0]
    earlier = one_hot(iota((step, step), 0) < iota((step, step), 1))
    ranks = []
    for t in range(STEPS):
        own = iota((512, step), 0) == block[:, t * step : (t + 1) * step]
        counts = jnp.dot(one_hot(own), earlier, preferred_element_type=f32)
        ranks.append(jnp.sum(jnp.where(own, counts, 0.0), axis=0, keepdims=True))
    rank = jnp.concatenate(ranks, axis=1).astype(i32)
    position = iota((1, tokens), 1)
    slot = jnp.where(position >= step, CAP, 0) + rank
    place = block * SLOTS + slot
    copies[1].wait()
    code = (offset_ref[...] + 1).astype(f32)
    lanes = jnp.where((iota((128, tokens), 0) & 7) == (place & 7), code, 0.0).astype(bf16)
    named = one_hot((iota((512, tokens), 0) >> 1) == (block >> 1))
    labels = lax.dot_general(named, lanes, NT, preferred_element_type=f32)
    labels = jnp.where((iota((512, 128), 0) & 1) == 1, pltpu.roll(labels, 4, 1), labels)
    labels = labels.reshape(64, 8, 128)
    digits = jnp.where(iota((8, tokens), 0) == 0, place >> 6, place & 63).astype(f32).astype(bf16)
    copies[2].wait()
    stored = one_hot(iota((tokens, tokens), 0) == order_ref[...])
    pair = lax.dot_general(digits, stored, NT, preferred_element_type=f32).astype(i32)
    place = pair[0:1] * 64 + pair[1:2]
    copies[3].wait()
    latents = latents_ref[...]
    chunk = 512
    low = iota((chunk // 8, 8, 128), 1) < 4
    groups = chunk // 32
    row = iota((groups, 8, 128), 1)
    for c in range(512 * SLOTS // chunk):
        pick = one_hot(iota((chunk, tokens), 0) + c * chunk == place)
        got = jnp.dot(pick, latents, preferred_element_type=f32)
        a = got[:, :128].reshape(chunk // 8, 8, 128)
        b = got[:, 128:].reshape(chunk // 8, 8, 128)
        first = jnp.where(low, a, pltpu.roll(b, 4, 1))
        second = jnp.where(low, pltpu.roll(a, 4, 1), b)
        m = jnp.stack([first, second], axis=1).reshape(groups, 4, 2, 8, 128)
        label = labels[c * groups : (c + 1) * groups]
        a1, b1 = pltpu.roll(m[:, 1, 0], 2, 1), pltpu.roll(m[:, 1, 1], 2, 1)
        a2, b2 = pltpu.roll(m[:, 2, 0], 4, 1), pltpu.roll(m[:, 2, 1], 4, 1)
        a3, b3 = pltpu.roll(m[:, 3, 0], 6, 1), pltpu.roll(m[:, 3, 1], 6, 1)
        tiles = [
            m[:, 0, 0],
            m[:, 0, 1],
            jnp.where(row < 2, label, a1),
            jnp.where(row < 2, a1, b1),
            jnp.where(row < 2, b1, jnp.where(row < 4, label, a2)),
            jnp.where(row < 4, a2, b2),
            jnp.where(row < 4, b2, jnp.where(row < 6, label, a3)),
            jnp.where(row < 6, a3, b3),
            jnp.where(row < 6, b3, label),
        ]
        count = groups * 72
        rows_ref[c * count : (c + 1) * count] = (
            jnp.stack(tiles, axis=1).reshape(count, 128).astype(bf16)
        )


def build(core, latents, order, block, offset):
    return pl.pallas_call(
        build_kernel,
        out_shape=jax.ShapeDtypeStruct((256 * 18, 128), bf16),
        in_specs=[pl.BlockSpec(memory_space=pltpu.SMEM)] + [pl.BlockSpec(memory_space=pltpu.HBM)] * 4,
        scratch_shapes=[
            pltpu.VMEM((1024, E), bf16),
            pltpu.VMEM((1, 1024), i32),
            pltpu.VMEM((1, 1024), i32),
            pltpu.VMEM((1, 1024), i32),
            pltpu.SemaphoreType.DMA((4,)),
        ],
        compiler_params=pltpu.CompilerParams(vmem_limit_bytes=60 << 20),
        cost_estimate=pl.CostEstimate(flops=3 << 30, bytes_accessed=2 << 20, transcendentals=0),
        name="build",
    )(core, latents, order, block, offset)


def partial_kernel(side, rows_ref, queries_ref, out_ref, hit_ref):
    del queries_ref
    tiles = rows_ref[...].astype(f32).reshape(64, 9, 8, 128)
    row = iota((64, 8, 128), 1)
    label = jnp.where(row < 6, tiles[:, 6], tiles[:, 8])
    label = jnp.where(row < 2, tiles[:, 2], jnp.where(row < 4, tiles[:, 4], label))
    line, lane = iota((64, 128), 0), iota((64, 128), 1)
    keep = line == 2 * (lane >> 2) + (((lane >> 2) & 1) ^ side)
    code = jnp.sum(jnp.where(keep, label.reshape(8, 64, 128), 0.0), axis=1).astype(i32)
    local = iota((2 * CPD, 128), 0)
    step = ((iota((2 * CPD, 128), 1) & 3) >> 1) == (local >> 8)
    local = jnp.where(step, (local & 255) + 1, -1)
    for i in range(8):
        hit_ref[:, i * 128 : (i + 1) * 128] = one_hot(local == code[i : i + 1])
    messages = []
    for i in range(4):
        at, shift = (18 * i + 8 * side) // 8, (18 * i) % 8
        if shift:
            low = pltpu.roll(tiles[:, at], 8 - shift, 1)
            high = pltpu.roll(tiles[:, at + 1], 8 - shift, 1)
            messages.append(jnp.where(row < 8 - shift, low, high))
        else:
            messages.append(tiles[:, at])
    first = jnp.stack(messages[0::2], axis=1).reshape(128, 8, 128)
    second = jnp.stack(messages[1::2], axis=1).reshape(128, 8, 128)
    low = iota((128, 8, 128), 1) < 4
    left = jnp.where(low, first, pltpu.roll(second, 4, 1)).reshape(1024, 128)
    right = jnp.where(low, pltpu.roll(first, 4, 1), second).reshape(1024, 128)
    rows = jnp.concatenate([left, right], axis=1).astype(bf16)
    hits = hit_ref[...]
    sums = jnp.dot(hits, rows, preferred_element_type=f32)
    counts = lax.dot_general(jnp.ones((8, 1024), bf16), hits, NT, preferred_element_type=f32)
    keep_rate, add_rate = ema_decay, 1.0 - ema_decay
    out_ref[:CPD] = keep_rate * (add_rate * sums[:CPD]) + add_rate * sums[CPD:]
    out_ref[CPD:] = keep_rate * (add_rate * counts[:, :CPD]) + add_rate * counts[:, CPD:]


def partial_update(side, rows, queries):
    return pl.pallas_call(
        functools.partial(partial_kernel, side),
        out_shape=jax.ShapeDtypeStruct((CPD + 8, E), f32),
        in_specs=[pl.BlockSpec(memory_space=pltpu.VMEM), pl.BlockSpec(memory_space=pl.ANY)],
        scratch_shapes=[pltpu.VMEM((2 * CPD, 1024), bf16)],
        compiler_params=pltpu.CompilerParams(vmem_limit_bytes=32 << 20),
        cost_estimate=pl.CostEstimate(flops=1 << 29, bytes_accessed=2 << 20, transcendentals=0),
        name="partial",
    )(rows, queries)


def merge_kernel(own_ref, other_ref, counts_ref, sums_ref, codebook_ref, new_counts_ref, new_sums_ref, rounded_ref):
    rows = own_ref[CPD:] + other_ref[CPD:]
    rows = ema_decay * (ema_decay * counts_ref[...]) + rows
    sums = ema_decay * (ema_decay * sums_ref[...]) + (own_ref[:CPD] + other_ref[:CPD])
    cols = jnp.transpose(jnp.broadcast_to(rows[0:1], (128, CPD)))
    book = jnp.concatenate([sums[:, :128] / cols, sums[:, 128:] / cols], axis=1)
    codebook_ref[...] = book
    rounded_ref[...] = book.astype(bf16)
    new_sums_ref[...] = sums
    new_counts_ref[...] = rows[0:1]


def merge(own, other, counts, sums):
    return pl.pallas_call(
        merge_kernel,
        out_shape=(
            jax.ShapeDtypeStruct((CPD, E), f32),
            jax.ShapeDtypeStruct((1, CPD), f32),
            jax.ShapeDtypeStruct((CPD, E), f32),
            jax.ShapeDtypeStruct((CPD, E), bf16),
        ),
        compiler_params=pltpu.CompilerParams(vmem_limit_bytes=32 << 20),
        cost_estimate=pl.CostEstimate(flops=1 << 20, bytes_accessed=2 << 20, transcendentals=0),
        name="merge",
    )(own, other, counts.reshape(1, CPD), sums)


def nearest_kernel(codes, *refs):
    groups, width = 16, 512
    codes_refs, queries_ref, rest = refs[:codes], refs[codes], refs[codes + 1 :]
    out_ref = rest[-1]
    last = out_ref.shape == (groups, 4, 128)
    scaled, norms = [], []
    for codes_ref in codes_refs:
        part = codes_ref[...].astype(f32)
        norms.append(jnp.sum(part * part, axis=1, keepdims=True))
        scaled.append((-2.0 * part).astype(bf16))
    for g in range(groups):
        part = queries_ref[g * width : (g + 1) * width]
        best = rest[0][g] if len(rest) > 1 else None
        for m, n in zip(scaled, norms):
            value = lax.dot_general(m, part, NT, preferred_element_type=f32) + n
            value = jnp.min(value.reshape(CPD // 8, 8, width), axis=0)
            best = value if best is None else jnp.minimum(best, value)
        if last:
            line = jnp.min(best, axis=0, keepdims=True)
            out_ref[g] = jnp.concatenate([line[:, j * 128 : (j + 1) * 128] for j in range(4)], axis=0)
        else:
            out_ref[g] = best


def nearest_codes(codes, queries, best=None, last=False):
    shape = (16, 4, 128) if last else (16, 8, 512)
    operands = (*codes, queries) if best is None else (*codes, queries, best)
    return pl.pallas_call(
        functools.partial(nearest_kernel, len(codes)),
        out_shape=jax.ShapeDtypeStruct(shape, f32),
        compiler_params=pltpu.CompilerParams(vmem_limit_bytes=32 << 20),
        cost_estimate=pl.CostEstimate(
            flops=len(codes) << 30, bytes_accessed=5 << 20, transcendentals=0
        ),
        name="nearest",
    )(*operands)


def swap_cores(x):
    return lax.ppermute(x, "core", [(0, 1), (1, 0)])


def body(latents, batch_order, code_block, code_offset, ema_counts, ema_sums, queries):
    core = lax.axis_index("core").astype(i32)
    half = queries.shape[0] // 2
    mine = lax.dynamic_slice_in_dim(queries, core * half, half, 0)
    plane_queries = lax.all_gather(mine, ("x", "y"), axis=0, tiled=True)
    own = jnp.sum(jnp.square(queries.astype(f32)), axis=1)
    rows = build(
        core.reshape(1), latents, batch_order, code_block.reshape(1, -1), code_offset.reshape(1, -1)
    )
    got = lax.all_to_all(rows.reshape(256, 9, 2, 128), ("zh", "x", "y", "zl"), 0, 0, tiled=True)
    got = got.reshape(256 * 18, 128)
    arrived = plane_queries[:16]
    other_part = swap_cores(partial_update(1, got, arrived))
    own_part = partial_update(0, got, arrived)
    codebook, counts, sums, rounded = merge(own_part, other_part, ema_counts, ema_sums)
    far = lax.ppermute(rounded, ("zh", "zl"), [(z, 15 - z) for z in range(16)])
    near_other = swap_cores(rounded)
    best = nearest_codes((rounded, near_other), plane_queries)
    far, best = lax.optimization_barrier((far, best))
    far_other = swap_cores(far)
    best = nearest_codes((far,), plane_queries, best)
    best = nearest_codes((far_other,), plane_queries, best, last=True)
    found = jnp.min(lax.all_to_all(best, ("x", "y"), 0, 0, tiled=True), axis=0)
    found = jnp.broadcast_to(found[None], (16, 4, 128))
    found = lax.all_to_all(found, ("zl", "core"), 0, 0, tiled=True)
    found = jnp.min(found.reshape(8, 2, 4, 128), axis=0).reshape(-1)
    nearest = (own + found) / E
    return (codebook, counts.reshape(-1), sums, nearest)


def solution(mesh):
    fine = Mesh(mesh.devices.reshape(SIZES), AXES)
    placed = (
        P(AXES, None),
        P(AXES, None),
        P(AXES, None),
        P(AXES),
        P(AXES),
        P(AXES, None),
        P(("zh", "x", "y"), None),
    )
    return jax.shard_map(
        body,
        mesh=fine,
        in_specs=placed,
        out_specs=(P(AXES, None), P(AXES), P(AXES, None), P(("zh", "x", "y"))),
        check_vma=False,
    )
```

```python
import functools

import jax
import jax.numpy as jnp
from jax import lax
from jax.experimental import pallas as pl
from jax.experimental.pallas import tpu as pltpu
from jax.sharding import Mesh, PartitionSpec as P

E = 256
CPD = 256
STEPS = 2
CAP = 2
SLOTS = STEPS * CAP
ema_decay = 0.9

AXES = ("zh", "x", "y", "zl", "core")
SIZES = (2, 4, 4, 8, 2)
NT = (((1,), (1,)), ((), ()))

f32 = jnp.float32
bf16 = jnp.bfloat16
i32 = jnp.int32


def iota(shape, dim):
    return lax.broadcasted_iota(i32, shape, dim)


def one_hot(hit):
    return jnp.where(hit, 1.0, 0.0).astype(bf16)


def build_kernel(core_ref, latents_hbm, order_hbm, block_hbm, offset_hbm, queries_hbm,
                 rows_ref, half_hbm, latents_ref, order_ref, block_ref, offset_ref, sems):
    tokens = latents_ref.shape[0]
    step = tokens // STEPS
    copies = [
        pltpu.make_async_copy(block_hbm, block_ref, sems.at[0]),
        pltpu.make_async_copy(offset_hbm, offset_ref, sems.at[1]),
        pltpu.make_async_copy(order_hbm, order_ref, sems.at[2]),
        pltpu.make_async_copy(latents_hbm, latents_ref, sems.at[3]),
    ]
    for copy in copies:
        copy.start()
    half = half_hbm.shape[0]
    side = pl.multiple_of(core_ref[0] * half, half)
    half_copy = pltpu.make_async_copy(queries_hbm.at[pl.ds(side, half)], half_hbm, sems.at[4])
    half_copy.start()
    copies[0].wait()
    block = block_ref[...] ^ core_ref[0]
    earlier = one_hot(iota((step, step), 0) < iota((step, step), 1))
    ranks = []
    for t in range(STEPS):
        own = iota((512, step), 0) == block[:, t * step : (t + 1) * step]
        counts = jnp.dot(one_hot(own), earlier, preferred_element_type=f32)
        ranks.append(jnp.sum(jnp.where(own, counts, 0.0), axis=0, keepdims=True))
    rank = jnp.concatenate(ranks, axis=1).astype(i32)
    position = iota((1, tokens), 1)
    slot = jnp.where(position >= step, CAP, 0) + rank
    place = block * SLOTS + slot
    copies[1].wait()
    code = (offset_ref[...] + 1).astype(f32)
    lanes = jnp.where((iota((128, tokens), 0) & 7) == (place & 7), code, 0.0).astype(bf16)
    named = one_hot((iota((512, tokens), 0) >> 1) == (block >> 1))
    labels = lax.dot_general(named, lanes, NT, preferred_element_type=f32)
    labels = jnp.where((iota((512, 128), 0) & 1) == 1, pltpu.roll(labels, 4, 1), labels)
    labels = labels.reshape(64, 8, 128)
    digits = jnp.where(iota((8, tokens), 0) == 0, place >> 6, place & 63).astype(f32).astype(bf16)
    copies[2].wait()
    stored = one_hot(iota((tokens, tokens), 0) == order_ref[...])
    pair = lax.dot_general(digits, stored, NT, preferred_element_type=f32).astype(i32)
    place = pair[0:1] * 64 + pair[1:2]
    copies[3].wait()
    latents = latents_ref[...]
    chunk = 512
    low = iota((chunk // 8, 8, 128), 1) < 4
    groups = chunk // 32
    row = iota((groups, 8, 128), 1)
    for c in range(512 * SLOTS // chunk):
        pick = one_hot(iota((chunk, tokens), 0) + c * chunk == place)
        got = jnp.dot(pick, latents, preferred_element_type=f32)
        a = got[:, :128].reshape(chunk // 8, 8, 128)
        b = got[:, 128:].reshape(chunk // 8, 8, 128)
        first = jnp.where(low, a, pltpu.roll(b, 4, 1))
        second = jnp.where(low, pltpu.roll(a, 4, 1), b)
        m = jnp.stack([first, second], axis=1).reshape(groups, 4, 2, 8, 128)
        label = labels[c * groups : (c + 1) * groups]
        a1, b1 = pltpu.roll(m[:, 1, 0], 2, 1), pltpu.roll(m[:, 1, 1], 2, 1)
        a2, b2 = pltpu.roll(m[:, 2, 0], 4, 1), pltpu.roll(m[:, 2, 1], 4, 1)
        a3, b3 = pltpu.roll(m[:, 3, 0], 6, 1), pltpu.roll(m[:, 3, 1], 6, 1)
        tiles = [
            m[:, 0, 0],
            m[:, 0, 1],
            jnp.where(row < 2, label, a1),
            jnp.where(row < 2, a1, b1),
            jnp.where(row < 2, b1, jnp.where(row < 4, label, a2)),
            jnp.where(row < 4, a2, b2),
            jnp.where(row < 4, b2, jnp.where(row < 6, label, a3)),
            jnp.where(row < 6, a3, b3),
            jnp.where(row < 6, b3, label),
        ]
        count = groups * 72
        rows_ref[c * count : (c + 1) * count] = (
            jnp.stack(tiles, axis=1).reshape(count, 128).astype(bf16)
        )
    half_copy.wait()


def build(core, latents, order, block, offset, queries):
    return pl.pallas_call(
        build_kernel,
        out_shape=(
            jax.ShapeDtypeStruct((256 * 18, 128), bf16),
            jax.ShapeDtypeStruct((512, E), bf16),
        ),
        in_specs=[pl.BlockSpec(memory_space=pltpu.SMEM)] + [pl.BlockSpec(memory_space=pltpu.HBM)] * 5,
        out_specs=(
            pl.BlockSpec(memory_space=pltpu.VMEM),
            pl.BlockSpec(memory_space=pltpu.HBM),
        ),
        scratch_shapes=[
            pltpu.VMEM((1024, E), bf16),
            pltpu.VMEM((1, 1024), i32),
            pltpu.VMEM((1, 1024), i32),
            pltpu.VMEM((1, 1024), i32),
            pltpu.SemaphoreType.DMA((5,)),
        ],
        compiler_params=pltpu.CompilerParams(vmem_limit_bytes=60 << 20),
        cost_estimate=pl.CostEstimate(flops=3 << 30, bytes_accessed=2 << 20, transcendentals=0),
        name="build",
    )(core, latents, order, block, offset, queries)


def partial_kernel(side, rows_ref, queries_ref, out_ref, hit_ref):
    del queries_ref
    tiles = rows_ref[...].astype(f32).reshape(64, 9, 8, 128)
    row = iota((64, 8, 128), 1)
    label = jnp.where(row < 6, tiles[:, 6], tiles[:, 8])
    label = jnp.where(row < 2, tiles[:, 2], jnp.where(row < 4, tiles[:, 4], label))
    line, lane = iota((64, 128), 0), iota((64, 128), 1)
    keep = line == 2 * (lane >> 2) + (((lane >> 2) & 1) ^ side)
    code = jnp.sum(jnp.where(keep, label.reshape(8, 64, 128), 0.0), axis=1).astype(i32)
    local = iota((2 * CPD, 128), 0)
    step = ((iota((2 * CPD, 128), 1) & 3) >> 1) == (local >> 8)
    local = jnp.where(step, (local & 255) + 1, -1)
    for i in range(8):
        hit_ref[:, i * 128 : (i + 1) * 128] = one_hot(local == code[i : i + 1])
    messages = []
    for i in range(4):
        at, shift = (18 * i + 8 * side) // 8, (18 * i) % 8
        if shift:
            low = pltpu.roll(tiles[:, at], 8 - shift, 1)
            high = pltpu.roll(tiles[:, at + 1], 8 - shift, 1)
            messages.append(jnp.where(row < 8 - shift, low, high))
        else:
            messages.append(tiles[:, at])
    first = jnp.stack(messages[0::2], axis=1).reshape(128, 8, 128)
    second = jnp.stack(messages[1::2], axis=1).reshape(128, 8, 128)
    low = iota((128, 8, 128), 1) < 4
    left = jnp.where(low, first, pltpu.roll(second, 4, 1)).reshape(1024, 128)
    right = jnp.where(low, pltpu.roll(first, 4, 1), second).reshape(1024, 128)
    rows = jnp.concatenate([left, right], axis=1).astype(bf16)
    hits = hit_ref[...]
    sums = jnp.dot(hits, rows, preferred_element_type=f32)
    counts = lax.dot_general(jnp.ones((8, 1024), bf16), hits, NT, preferred_element_type=f32)
    keep_rate, add_rate = ema_decay, 1.0 - ema_decay
    out_ref[:CPD] = keep_rate * (add_rate * sums[:CPD]) + add_rate * sums[CPD:]
    out_ref[CPD:] = keep_rate * (add_rate * counts[:, :CPD]) + add_rate * counts[:, CPD:]


def partial_update(side, rows, queries):
    return pl.pallas_call(
        functools.partial(partial_kernel, side),
        out_shape=jax.ShapeDtypeStruct((CPD + 8, E), f32),
        in_specs=[pl.BlockSpec(memory_space=pltpu.VMEM), pl.BlockSpec(memory_space=pl.ANY)],
        scratch_shapes=[pltpu.VMEM((2 * CPD, 1024), bf16)],
        compiler_params=pltpu.CompilerParams(vmem_limit_bytes=32 << 20),
        cost_estimate=pl.CostEstimate(flops=1 << 29, bytes_accessed=2 << 20, transcendentals=0),
        name="partial",
    )(rows, queries)


def merge_kernel(own_ref, other_ref, counts_ref, sums_ref, codebook_ref, new_counts_ref, new_sums_ref, rounded_ref):
    rows = own_ref[CPD:] + other_ref[CPD:]
    rows = ema_decay * (ema_decay * counts_ref[...]) + rows
    sums = ema_decay * (ema_decay * sums_ref[...]) + (own_ref[:CPD] + other_ref[:CPD])
    cols = jnp.transpose(jnp.broadcast_to(rows[0:1], (128, CPD)))
    book = jnp.concatenate([sums[:, :128] / cols, sums[:, 128:] / cols], axis=1)
    codebook_ref[...] = book
    rounded_ref[...] = book.astype(bf16)
    new_sums_ref[...] = sums
    new_counts_ref[...] = rows[0:1]


def merge(own, other, counts, sums):
    return pl.pallas_call(
        merge_kernel,
        out_shape=(
            jax.ShapeDtypeStruct((CPD, E), f32),
            jax.ShapeDtypeStruct((1, CPD), f32),
            jax.ShapeDtypeStruct((CPD, E), f32),
            jax.ShapeDtypeStruct((CPD, E), bf16),
        ),
        compiler_params=pltpu.CompilerParams(vmem_limit_bytes=32 << 20),
        cost_estimate=pl.CostEstimate(flops=1 << 20, bytes_accessed=2 << 20, transcendentals=0),
        name="merge",
    )(own, other, counts.reshape(1, CPD), sums)


def nearest_kernel(codes, *refs):
    groups, width = 16, 512
    codes_refs, queries_ref, rest = refs[:codes], refs[codes], refs[codes + 1 :]
    out_ref = rest[-1]
    last = out_ref.shape == (groups, 4, 128)
    scaled, norms = [], []
    for codes_ref in codes_refs:
        part = codes_ref[...].astype(f32)
        norms.append(jnp.sum(part * part, axis=1, keepdims=True))
        scaled.append((-2.0 * part).astype(bf16))
    for g in range(groups):
        part = queries_ref[g * width : (g + 1) * width]
        best = rest[0][g] if len(rest) > 1 else None
        for m, n in zip(scaled, norms):
            value = lax.dot_general(m, part, NT, preferred_element_type=f32) + n
            value = jnp.min(value.reshape(-1, 8, width), axis=0)
            best = value if best is None else jnp.minimum(best, value)
        if last:
            line = jnp.min(best, axis=0, keepdims=True)
            out_ref[g] = jnp.concatenate([line[:, j * 128 : (j + 1) * 128] for j in range(4)], axis=0)
        else:
            out_ref[g] = best


def nearest_codes(codes, queries, best=None, last=False):
    shape = (16, 4, 128) if last else (16, 8, 512)
    operands = (*codes, queries) if best is None else (*codes, queries, best)
    return pl.pallas_call(
        functools.partial(nearest_kernel, len(codes)),
        out_shape=jax.ShapeDtypeStruct(shape, f32),
        compiler_params=pltpu.CompilerParams(vmem_limit_bytes=32 << 20),
        cost_estimate=pl.CostEstimate(
            flops=len(codes) << 30, bytes_accessed=5 << 20, transcendentals=0
        ),
        name="nearest",
    )(*operands)


def swap_cores(x):
    return lax.ppermute(x, "core", [(0, 1), (1, 0)])


def body(latents, batch_order, code_block, code_offset, ema_counts, ema_sums, queries):
    core = lax.axis_index("core").astype(i32)
    own = jnp.sum(jnp.square(queries.astype(f32)), axis=1)
    rows, mine = build(
        core.reshape(1),
        latents,
        batch_order,
        code_block.reshape(1, -1),
        code_offset.reshape(1, -1),
        queries,
    )
    plane_queries = lax.all_gather(mine, ("x", "y"), axis=0, tiled=True)
    got = lax.all_to_all(rows.reshape(256, 9, 2, 128), ("zh", "x", "y", "zl"), 0, 0, tiled=True)
    got = got.reshape(256 * 18, 128)
    arrived = plane_queries[:16]
    other_part = swap_cores(partial_update(1, got, arrived))
    own_part = partial_update(0, got, arrived)
    codebook, counts, sums, rounded = merge(own_part, other_part, ema_counts, ema_sums)
    far = lax.ppermute(rounded, ("zh", "zl"), [(z, 15 - z) for z in range(16)])
    near = lax.all_gather(rounded, "core", axis=0, tiled=True)
    best = nearest_codes((near,), plane_queries)
    far, best = lax.optimization_barrier((far, best))
    far_other = swap_cores(far)
    best = nearest_codes((far,), plane_queries, best)
    best = nearest_codes((far_other,), plane_queries, best, last=True)
    found = jnp.min(lax.all_to_all(best, ("x", "y"), 0, 0, tiled=True), axis=0)
    found = jnp.broadcast_to(found[None], (16, 4, 128))
    found = lax.all_to_all(found, ("zl", "core"), 0, 0, tiled=True)
    found = jnp.min(found.reshape(8, 2, 4, 128), axis=0).reshape(-1)
    nearest = (own + found) / E
    return (codebook, counts.reshape(-1), sums, nearest)


def solution(mesh):
    fine = Mesh(mesh.devices.reshape(SIZES), AXES)
    placed = (
        P(AXES, None),
        P(AXES, None),
        P(AXES, None),
        P(AXES),
        P(AXES),
        P(AXES, None),
        P(("zh", "x", "y"), None),
    )
    return jax.shard_map(
        body,
        mesh=fine,
        in_specs=placed,
        out_specs=(P(AXES, None), P(AXES), P(AXES, None), P(("zh", "x", "y"))),
        check_vma=False,
    )
```

```python
import functools

import jax
import jax.numpy as jnp
from jax import lax
from jax.experimental import pallas as pl
from jax.experimental.pallas import tpu as pltpu
from jax.sharding import Mesh, PartitionSpec as P

E = 256
CPD = 256
STEPS = 2
CAP = 2
SLOTS = STEPS * CAP
ema_decay = 0.9

AXES = ("zh", "x", "y", "zl", "core")
SIZES = (2, 4, 4, 8, 2)
NT = (((1,), (1,)), ((), ()))

f32 = jnp.float32
bf16 = jnp.bfloat16
i32 = jnp.int32


def iota(shape, dim):
    return lax.broadcasted_iota(i32, shape, dim)


def one_hot(hit):
    return jnp.where(hit, 1.0, 0.0).astype(bf16)


def build_kernel(core_ref, latents_hbm, order_hbm, block_hbm, offset_hbm, queries_hbm,
                 rows_ref, half_hbm, half_ref, latents_ref, order_ref,
                 block_ref, offset_ref, sems):
    tokens = latents_ref.shape[0]
    step = tokens // STEPS
    copies = [
        pltpu.make_async_copy(block_hbm, block_ref, sems.at[0]),
        pltpu.make_async_copy(offset_hbm, offset_ref, sems.at[1]),
        pltpu.make_async_copy(order_hbm, order_ref, sems.at[2]),
        pltpu.make_async_copy(latents_hbm, latents_ref, sems.at[3]),
    ]
    for copy in copies:
        copy.start()
    half = half_hbm.shape[0]
    side = pl.multiple_of(core_ref[0] * half, half)
    half_in = pltpu.make_async_copy(queries_hbm.at[pl.ds(side, half)], half_ref, sems.at[4])
    half_in.start()
    copies[0].wait()
    block = block_ref[...] ^ core_ref[0]
    earlier = one_hot(iota((step, step), 0) < iota((step, step), 1))
    ranks = []
    for t in range(STEPS):
        own = iota((512, step), 0) == block[:, t * step : (t + 1) * step]
        counts = jnp.dot(one_hot(own), earlier, preferred_element_type=f32)
        ranks.append(jnp.sum(jnp.where(own, counts, 0.0), axis=0, keepdims=True))
    rank = jnp.concatenate(ranks, axis=1).astype(i32)
    position = iota((1, tokens), 1)
    slot = jnp.where(position >= step, CAP, 0) + rank
    place = block * SLOTS + slot
    copies[1].wait()
    code = (offset_ref[...] + 1).astype(f32)
    lanes = jnp.where((iota((128, tokens), 0) & 7) == (place & 7), code, 0.0).astype(bf16)
    named = one_hot((iota((512, tokens), 0) >> 1) == (block >> 1))
    labels = lax.dot_general(named, lanes, NT, preferred_element_type=f32)
    labels = jnp.where((iota((512, 128), 0) & 1) == 1, pltpu.roll(labels, 4, 1), labels)
    labels = labels.reshape(64, 8, 128)
    half_in.wait()
    half_out = pltpu.make_async_copy(half_ref, half_hbm, sems.at[5])
    half_out.start()
    digits = jnp.where(iota((8, tokens), 0) == 0, place >> 6, place & 63).astype(f32).astype(bf16)
    copies[2].wait()
    stored = one_hot(iota((tokens, tokens), 0) == order_ref[...])
    pair = lax.dot_general(digits, stored, NT, preferred_element_type=f32).astype(i32)
    place = pair[0:1] * 64 + pair[1:2]
    copies[3].wait()
    latents = latents_ref[...]
    chunk = 512
    low = iota((chunk // 8, 8, 128), 1) < 4
    groups = chunk // 32
    row = iota((groups, 8, 128), 1)
    for c in range(512 * SLOTS // chunk):
        pick = one_hot(iota((chunk, tokens), 0) + c * chunk == place)
        got = jnp.dot(pick, latents, preferred_element_type=f32)
        a = got[:, :128].reshape(chunk // 8, 8, 128)
        b = got[:, 128:].reshape(chunk // 8, 8, 128)
        first = jnp.where(low, a, pltpu.roll(b, 4, 1))
        second = jnp.where(low, pltpu.roll(a, 4, 1), b)
        m = jnp.stack([first, second], axis=1).reshape(groups, 4, 2, 8, 128)
        label = labels[c * groups : (c + 1) * groups]
        a1, b1 = pltpu.roll(m[:, 1, 0], 2, 1), pltpu.roll(m[:, 1, 1], 2, 1)
        a2, b2 = pltpu.roll(m[:, 2, 0], 4, 1), pltpu.roll(m[:, 2, 1], 4, 1)
        a3, b3 = pltpu.roll(m[:, 3, 0], 6, 1), pltpu.roll(m[:, 3, 1], 6, 1)
        tiles = [
            m[:, 0, 0],
            m[:, 0, 1],
            jnp.where(row < 2, label, a1),
            jnp.where(row < 2, a1, b1),
            jnp.where(row < 2, b1, jnp.where(row < 4, label, a2)),
            jnp.where(row < 4, a2, b2),
            jnp.where(row < 4, b2, jnp.where(row < 6, label, a3)),
            jnp.where(row < 6, a3, b3),
            jnp.where(row < 6, b3, label),
        ]
        count = groups * 72
        rows_ref[c * count : (c + 1) * count] = (
            jnp.stack(tiles, axis=1).reshape(count, 128).astype(bf16)
        )
    half_out.wait()


def build(core, latents, order, block, offset, queries):
    return pl.pallas_call(
        build_kernel,
        out_shape=(
            jax.ShapeDtypeStruct((256 * 18, 128), bf16),
            jax.ShapeDtypeStruct((512, E), bf16),
        ),
        in_specs=[pl.BlockSpec(memory_space=pltpu.SMEM)] + [pl.BlockSpec(memory_space=pltpu.HBM)] * 5,
        out_specs=(
            pl.BlockSpec(memory_space=pltpu.VMEM),
            pl.BlockSpec(memory_space=pltpu.HBM),
        ),
        scratch_shapes=[
            pltpu.VMEM((512, E), bf16),
            pltpu.VMEM((1024, E), bf16),
            pltpu.VMEM((1, 1024), i32),
            pltpu.VMEM((1, 1024), i32),
            pltpu.VMEM((1, 1024), i32),
            pltpu.SemaphoreType.DMA((6,)),
        ],
        compiler_params=pltpu.CompilerParams(vmem_limit_bytes=60 << 20),
        cost_estimate=pl.CostEstimate(flops=3 << 30, bytes_accessed=2 << 20, transcendentals=0),
        name="build",
    )(core, latents, order, block, offset, queries)


def partial_kernel(side, rows_ref, queries_ref, out_ref, hit_ref):
    del queries_ref
    tiles = rows_ref[...].astype(f32).reshape(64, 9, 8, 128)
    row = iota((64, 8, 128), 1)
    label = jnp.where(row < 6, tiles[:, 6], tiles[:, 8])
    label = jnp.where(row < 2, tiles[:, 2], jnp.where(row < 4, tiles[:, 4], label))
    line, lane = iota((64, 128), 0), iota((64, 128), 1)
    keep = line == 2 * (lane >> 2) + (((lane >> 2) & 1) ^ side)
    code = jnp.sum(jnp.where(keep, label.reshape(8, 64, 128), 0.0), axis=1).astype(i32)
    local = iota((2 * CPD, 128), 0)
    step = ((iota((2 * CPD, 128), 1) & 3) >> 1) == (local >> 8)
    local = jnp.where(step, (local & 255) + 1, -1)
    for i in range(8):
        hit_ref[:, i * 128 : (i + 1) * 128] = one_hot(local == code[i : i + 1])
    messages = []
    for i in range(4):
        at, shift = (18 * i + 8 * side) // 8, (18 * i) % 8
        if shift:
            low = pltpu.roll(tiles[:, at], 8 - shift, 1)
            high = pltpu.roll(tiles[:, at + 1], 8 - shift, 1)
            messages.append(jnp.where(row < 8 - shift, low, high))
        else:
            messages.append(tiles[:, at])
    first = jnp.stack(messages[0::2], axis=1).reshape(128, 8, 128)
    second = jnp.stack(messages[1::2], axis=1).reshape(128, 8, 128)
    low = iota((128, 8, 128), 1) < 4
    left = jnp.where(low, first, pltpu.roll(second, 4, 1)).reshape(1024, 128)
    right = jnp.where(low, pltpu.roll(first, 4, 1), second).reshape(1024, 128)
    rows = jnp.concatenate([left, right], axis=1).astype(bf16)
    hits = hit_ref[...]
    sums = jnp.dot(hits, rows, preferred_element_type=f32)
    counts = lax.dot_general(jnp.ones((8, 1024), bf16), hits, NT, preferred_element_type=f32)
    keep_rate, add_rate = ema_decay, 1.0 - ema_decay
    out_ref[:CPD] = keep_rate * (add_rate * sums[:CPD]) + add_rate * sums[CPD:]
    out_ref[CPD:] = keep_rate * (add_rate * counts[:, :CPD]) + add_rate * counts[:, CPD:]


def partial_update(side, rows, queries):
    return pl.pallas_call(
        functools.partial(partial_kernel, side),
        out_shape=jax.ShapeDtypeStruct((CPD + 8, E), f32),
        in_specs=[pl.BlockSpec(memory_space=pltpu.VMEM), pl.BlockSpec(memory_space=pl.ANY)],
        scratch_shapes=[pltpu.VMEM((2 * CPD, 1024), bf16)],
        compiler_params=pltpu.CompilerParams(vmem_limit_bytes=32 << 20),
        cost_estimate=pl.CostEstimate(flops=1 << 29, bytes_accessed=2 << 20, transcendentals=0),
        name="partial",
    )(rows, queries)


def merge_kernel(own_ref, other_ref, counts_ref, sums_ref, codebook_ref, new_counts_ref, new_sums_ref, rounded_ref):
    rows = own_ref[CPD:] + other_ref[CPD:]
    rows = ema_decay * (ema_decay * counts_ref[...]) + rows
    sums = ema_decay * (ema_decay * sums_ref[...]) + (own_ref[:CPD] + other_ref[:CPD])
    cols = jnp.transpose(jnp.broadcast_to(rows[0:1], (128, CPD)))
    book = jnp.concatenate([sums[:, :128] / cols, sums[:, 128:] / cols], axis=1)
    codebook_ref[...] = book
    rounded_ref[...] = book.astype(bf16)
    new_sums_ref[...] = sums
    new_counts_ref[...] = rows[0:1]


def merge(own, other, counts, sums):
    return pl.pallas_call(
        merge_kernel,
        out_shape=(
            jax.ShapeDtypeStruct((CPD, E), f32),
            jax.ShapeDtypeStruct((1, CPD), f32),
            jax.ShapeDtypeStruct((CPD, E), f32),
            jax.ShapeDtypeStruct((CPD, E), bf16),
        ),
        compiler_params=pltpu.CompilerParams(vmem_limit_bytes=32 << 20),
        cost_estimate=pl.CostEstimate(flops=1 << 20, bytes_accessed=2 << 20, transcendentals=0),
        name="merge",
    )(own, other, counts.reshape(1, CPD), sums)


def nearest_kernel(codes, *refs):
    groups, width = 16, 512
    codes_refs, queries_ref, rest = refs[:codes], refs[codes], refs[codes + 1 :]
    out_ref = rest[-1]
    last = out_ref.shape == (groups, 4, 128)
    scaled, norms = [], []
    for codes_ref in codes_refs:
        part = codes_ref[...].astype(f32)
        norms.append(jnp.sum(part * part, axis=1, keepdims=True))
        scaled.append((-2.0 * part).astype(bf16))
    for g in range(groups):
        part = queries_ref[g * width : (g + 1) * width]
        best = rest[0][g] if len(rest) > 1 else None
        for m, n in zip(scaled, norms):
            value = lax.dot_general(m, part, NT, preferred_element_type=f32) + n
            value = jnp.min(value.reshape(-1, 8, width), axis=0)
            best = value if best is None else jnp.minimum(best, value)
        if last:
            line = jnp.min(best, axis=0, keepdims=True)
            out_ref[g] = jnp.concatenate([line[:, j * 128 : (j + 1) * 128] for j in range(4)], axis=0)
        else:
            out_ref[g] = best


def nearest_codes(codes, queries, best=None, last=False):
    shape = (16, 4, 128) if last else (16, 8, 512)
    operands = (*codes, queries) if best is None else (*codes, queries, best)
    return pl.pallas_call(
        functools.partial(nearest_kernel, len(codes)),
        out_shape=jax.ShapeDtypeStruct(shape, f32),
        compiler_params=pltpu.CompilerParams(vmem_limit_bytes=32 << 20),
        cost_estimate=pl.CostEstimate(
            flops=len(codes) << 30, bytes_accessed=5 << 20, transcendentals=0
        ),
        name="nearest",
    )(*operands)


def swap_cores(x):
    return lax.ppermute(x, "core", [(0, 1), (1, 0)])


def body(latents, batch_order, code_block, code_offset, ema_counts, ema_sums, queries):
    core = lax.axis_index("core").astype(i32)
    own = jnp.sum(jnp.square(queries.astype(f32)), axis=1)
    rows, mine = build(
        core.reshape(1),
        latents,
        batch_order,
        code_block.reshape(1, -1),
        code_offset.reshape(1, -1),
        queries,
    )
    plane_queries = lax.all_gather(mine, ("x", "y"), axis=0, tiled=True)
    got = lax.all_to_all(rows.reshape(256, 9, 2, 128), ("zh", "x", "y", "zl"), 0, 0, tiled=True)
    got = got.reshape(256 * 18, 128)
    arrived = plane_queries[:16]
    other_part = swap_cores(partial_update(1, got, arrived))
    own_part = partial_update(0, got, arrived)
    codebook, counts, sums, rounded = merge(own_part, other_part, ema_counts, ema_sums)
    far = lax.ppermute(rounded, ("zh", "zl"), [(z, 15 - z) for z in range(16)])
    near = lax.all_gather(rounded, "core", axis=0, tiled=True)
    best = nearest_codes((near,), plane_queries)
    far, best = lax.optimization_barrier((far, best))
    far_other = swap_cores(far)
    best = nearest_codes((far,), plane_queries, best)
    best = nearest_codes((far_other,), plane_queries, best, last=True)
    found = jnp.min(lax.all_to_all(best, ("x", "y"), 0, 0, tiled=True), axis=0)
    found = jnp.broadcast_to(found[None], (16, 4, 128))
    found = lax.all_to_all(found, ("zl", "core"), 0, 0, tiled=True)
    found = jnp.min(found.reshape(8, 2, 4, 128), axis=0).reshape(-1)
    nearest = (own + found) / E
    return (codebook, counts.reshape(-1), sums, nearest)


def solution(mesh):
    fine = Mesh(mesh.devices.reshape(SIZES), AXES)
    placed = (
        P(AXES, None),
        P(AXES, None),
        P(AXES, None),
        P(AXES),
        P(AXES),
        P(AXES, None),
        P(("zh", "x", "y"), None),
    )
    return jax.shard_map(
        body,
        mesh=fine,
        in_specs=placed,
        out_specs=(P(AXES, None), P(AXES), P(AXES, None), P(("zh", "x", "y"))),
        check_vma=False,
    )
```

```python
import functools

import jax
import jax.numpy as jnp
from jax import lax
from jax.experimental import pallas as pl
from jax.experimental.pallas import tpu as pltpu
from jax.sharding import Mesh, PartitionSpec as P

E = 256
CPD = 256
STEPS = 2
CAP = 2
SLOTS = STEPS * CAP
ema_decay = 0.9

AXES = ("zh", "xa", "xb", "y", "zl", "core")
SIZES = (2, 2, 2, 4, 8, 2)
NT = (((1,), (1,)), ((), ()))

f32 = jnp.float32
bf16 = jnp.bfloat16
i32 = jnp.int32


def iota(shape, dim):
    return lax.broadcasted_iota(i32, shape, dim)


def one_hot(hit):
    return jnp.where(hit, 1.0, 0.0).astype(bf16)


def build_kernel(core_ref, latents_hbm, order_hbm, block_hbm, offset_hbm, queries_hbm,
                 rows_ref, half_hbm, half_ref, latents_ref, order_ref,
                 block_ref, offset_ref, sems):
    tokens = latents_ref.shape[0]
    step = tokens // STEPS
    copies = [
        pltpu.make_async_copy(block_hbm, block_ref, sems.at[0]),
        pltpu.make_async_copy(offset_hbm, offset_ref, sems.at[1]),
        pltpu.make_async_copy(order_hbm, order_ref, sems.at[2]),
        pltpu.make_async_copy(latents_hbm, latents_ref, sems.at[3]),
    ]
    for copy in copies:
        copy.start()
    half = half_hbm.shape[0]
    side = pl.multiple_of(core_ref[0] * half, half)
    half_in = pltpu.make_async_copy(queries_hbm.at[pl.ds(side, half)], half_ref, sems.at[4])
    half_in.start()
    copies[0].wait()
    block = block_ref[...] ^ core_ref[0]
    earlier = one_hot(iota((step, step), 0) < iota((step, step), 1))
    ranks = []
    for t in range(STEPS):
        own = iota((512, step), 0) == block[:, t * step : (t + 1) * step]
        counts = jnp.dot(one_hot(own), earlier, preferred_element_type=f32)
        ranks.append(jnp.sum(jnp.where(own, counts, 0.0), axis=0, keepdims=True))
    rank = jnp.concatenate(ranks, axis=1).astype(i32)
    position = iota((1, tokens), 1)
    slot = jnp.where(position >= step, CAP, 0) + rank
    place = block * SLOTS + slot
    copies[1].wait()
    code = (offset_ref[...] + 1).astype(f32)
    lanes = jnp.where((iota((128, tokens), 0) & 7) == (place & 7), code, 0.0).astype(bf16)
    named = one_hot((iota((512, tokens), 0) >> 1) == (block >> 1))
    labels = lax.dot_general(named, lanes, NT, preferred_element_type=f32)
    labels = jnp.where((iota((512, 128), 0) & 1) == 1, pltpu.roll(labels, 4, 1), labels)
    labels = labels.reshape(64, 8, 128)
    half_in.wait()
    half_out = pltpu.make_async_copy(half_ref, half_hbm, sems.at[5])
    half_out.start()
    digits = jnp.where(iota((8, tokens), 0) == 0, place >> 6, place & 63).astype(f32).astype(bf16)
    copies[2].wait()
    stored = one_hot(iota((tokens, tokens), 0) == order_ref[...])
    pair = lax.dot_general(digits, stored, NT, preferred_element_type=f32).astype(i32)
    place = pair[0:1] * 64 + pair[1:2]
    copies[3].wait()
    latents = latents_ref[...]
    chunk = 512
    low = iota((chunk // 8, 8, 128), 1) < 4
    groups = chunk // 32
    row = iota((groups, 8, 128), 1)
    for c in range(512 * SLOTS // chunk):
        pick = one_hot(iota((chunk, tokens), 0) + c * chunk == place)
        got = jnp.dot(pick, latents, preferred_element_type=f32)
        a = got[:, :128].reshape(chunk // 8, 8, 128)
        b = got[:, 128:].reshape(chunk // 8, 8, 128)
        first = jnp.where(low, a, pltpu.roll(b, 4, 1))
        second = jnp.where(low, pltpu.roll(a, 4, 1), b)
        m = jnp.stack([first, second], axis=1).reshape(groups, 4, 2, 8, 128)
        label = labels[c * groups : (c + 1) * groups]
        a1, b1 = pltpu.roll(m[:, 1, 0], 2, 1), pltpu.roll(m[:, 1, 1], 2, 1)
        a2, b2 = pltpu.roll(m[:, 2, 0], 4, 1), pltpu.roll(m[:, 2, 1], 4, 1)
        a3, b3 = pltpu.roll(m[:, 3, 0], 6, 1), pltpu.roll(m[:, 3, 1], 6, 1)
        tiles = [
            m[:, 0, 0],
            m[:, 0, 1],
            jnp.where(row < 2, label, a1),
            jnp.where(row < 2, a1, b1),
            jnp.where(row < 2, b1, jnp.where(row < 4, label, a2)),
            jnp.where(row < 4, a2, b2),
            jnp.where(row < 4, b2, jnp.where(row < 6, label, a3)),
            jnp.where(row < 6, a3, b3),
            jnp.where(row < 6, b3, label),
        ]
        count = groups * 72
        rows_ref[c * count : (c + 1) * count] = (
            jnp.stack(tiles, axis=1).reshape(count, 128).astype(bf16)
        )
    half_out.wait()


def build(core, latents, order, block, offset, queries):
    return pl.pallas_call(
        build_kernel,
        out_shape=(
            jax.ShapeDtypeStruct((256 * 18, 128), bf16),
            jax.ShapeDtypeStruct((512, E), bf16),
        ),
        in_specs=[pl.BlockSpec(memory_space=pltpu.SMEM)] + [pl.BlockSpec(memory_space=pltpu.HBM)] * 5,
        out_specs=(
            pl.BlockSpec(memory_space=pltpu.VMEM),
            pl.BlockSpec(memory_space=pltpu.HBM),
        ),
        scratch_shapes=[
            pltpu.VMEM((512, E), bf16),
            pltpu.VMEM((1024, E), bf16),
            pltpu.VMEM((1, 1024), i32),
            pltpu.VMEM((1, 1024), i32),
            pltpu.VMEM((1, 1024), i32),
            pltpu.SemaphoreType.DMA((6,)),
        ],
        compiler_params=pltpu.CompilerParams(vmem_limit_bytes=60 << 20),
        cost_estimate=pl.CostEstimate(flops=3 << 30, bytes_accessed=2 << 20, transcendentals=0),
        name="build",
    )(core, latents, order, block, offset, queries)


def partial_kernel(side, rows_ref, queries_ref, out_ref, hit_ref):
    del queries_ref
    tiles = rows_ref[...].astype(f32).reshape(64, 9, 8, 128)
    row = iota((64, 8, 128), 1)
    label = jnp.where(row < 6, tiles[:, 6], tiles[:, 8])
    label = jnp.where(row < 2, tiles[:, 2], jnp.where(row < 4, tiles[:, 4], label))
    line, lane = iota((64, 128), 0), iota((64, 128), 1)
    keep = line == 2 * (lane >> 2) + (((lane >> 2) & 1) ^ side)
    code = jnp.sum(jnp.where(keep, label.reshape(8, 64, 128), 0.0), axis=1).astype(i32)
    local = iota((2 * CPD, 128), 0)
    step = ((iota((2 * CPD, 128), 1) & 3) >> 1) == (local >> 8)
    local = jnp.where(step, (local & 255) + 1, -1)
    for i in range(8):
        hit_ref[:, i * 128 : (i + 1) * 128] = one_hot(local == code[i : i + 1])
    messages = []
    for i in range(4):
        at, shift = (18 * i + 8 * side) // 8, (18 * i) % 8
        if shift:
            low = pltpu.roll(tiles[:, at], 8 - shift, 1)
            high = pltpu.roll(tiles[:, at + 1], 8 - shift, 1)
            messages.append(jnp.where(row < 8 - shift, low, high))
        else:
            messages.append(tiles[:, at])
    first = jnp.stack(messages[0::2], axis=1).reshape(128, 8, 128)
    second = jnp.stack(messages[1::2], axis=1).reshape(128, 8, 128)
    low = iota((128, 8, 128), 1) < 4
    left = jnp.where(low, first, pltpu.roll(second, 4, 1)).reshape(1024, 128)
    right = jnp.where(low, pltpu.roll(first, 4, 1), second).reshape(1024, 128)
    rows = jnp.concatenate([left, right], axis=1).astype(bf16)
    hits = hit_ref[...]
    sums = jnp.dot(hits, rows, preferred_element_type=f32)
    counts = lax.dot_general(jnp.ones((8, 1024), bf16), hits, NT, preferred_element_type=f32)
    keep_rate, add_rate = ema_decay, 1.0 - ema_decay
    out_ref[:CPD] = keep_rate * (add_rate * sums[:CPD]) + add_rate * sums[CPD:]
    out_ref[CPD:] = keep_rate * (add_rate * counts[:, :CPD]) + add_rate * counts[:, CPD:]


def partial_update(side, rows, queries):
    return pl.pallas_call(
        functools.partial(partial_kernel, side),
        out_shape=jax.ShapeDtypeStruct((CPD + 8, E), f32),
        in_specs=[pl.BlockSpec(memory_space=pltpu.VMEM), pl.BlockSpec(memory_space=pl.ANY)],
        scratch_shapes=[pltpu.VMEM((2 * CPD, 1024), bf16)],
        compiler_params=pltpu.CompilerParams(vmem_limit_bytes=32 << 20),
        cost_estimate=pl.CostEstimate(flops=1 << 29, bytes_accessed=2 << 20, transcendentals=0),
        name="partial",
    )(rows, queries)


def merge_kernel(own_ref, other_ref, counts_ref, sums_ref, codebook_ref, new_counts_ref, new_sums_ref, rounded_ref):
    rows = own_ref[CPD:] + other_ref[CPD:]
    rows = ema_decay * (ema_decay * counts_ref[...]) + rows
    sums = ema_decay * (ema_decay * sums_ref[...]) + (own_ref[:CPD] + other_ref[:CPD])
    cols = jnp.transpose(jnp.broadcast_to(rows[0:1], (128, CPD)))
    book = jnp.concatenate([sums[:, :128] / cols, sums[:, 128:] / cols], axis=1)
    codebook_ref[...] = book
    rounded_ref[...] = book.astype(bf16)
    new_sums_ref[...] = sums
    new_counts_ref[...] = rows[0:1]


def merge(own, other, counts, sums):
    return pl.pallas_call(
        merge_kernel,
        out_shape=(
            jax.ShapeDtypeStruct((CPD, E), f32),
            jax.ShapeDtypeStruct((1, CPD), f32),
            jax.ShapeDtypeStruct((CPD, E), f32),
            jax.ShapeDtypeStruct((CPD, E), bf16),
        ),
        compiler_params=pltpu.CompilerParams(vmem_limit_bytes=32 << 20),
        cost_estimate=pl.CostEstimate(flops=1 << 20, bytes_accessed=2 << 20, transcendentals=0),
        name="merge",
    )(own, other, counts.reshape(1, CPD), sums)


PIECES = (176, 176, 160)


def stage_kernel(*refs):
    out_ref = refs[-1]
    at = 0
    for ref, rows in zip(refs[:-1], PIECES):
        for g in range(8):
            out_ref[g * 512 + at : g * 512 + at + rows] = ref[g * rows : (g + 1) * rows]
        at += rows


def stage(pieces):
    return pl.pallas_call(
        stage_kernel,
        out_shape=jax.ShapeDtypeStruct((8 * 512, E), bf16),
        compiler_params=pltpu.CompilerParams(vmem_limit_bytes=32 << 20),
        name="stage",
    )(*pieces)


def nearest_kernel(codes_ref, queries_ref, *refs):
    groups, width = 8, 512
    out_ref = refs[-1]
    last = out_ref.shape == (groups, 4, 128)
    scaled, norms = [], []
    for c in range(codes_ref.shape[0] // CPD):
        part = codes_ref[c * CPD : (c + 1) * CPD].astype(f32)
        norms.append(jnp.sum(part * part, axis=1, keepdims=True))
        scaled.append((-2.0 * part).astype(bf16))
    for g in range(groups):
        part = queries_ref[g * width : (g + 1) * width]
        best = refs[0][g] if len(refs) > 1 else None
        for m, n in zip(scaled, norms):
            value = lax.dot_general(m, part, NT, preferred_element_type=f32) + n
            value = jnp.min(value.reshape(CPD // 8, 8, width), axis=0)
            best = value if best is None else jnp.minimum(best, value)
        if last:
            line = jnp.min(best, axis=0, keepdims=True)
            out_ref[g] = jnp.concatenate([line[:, j * 128 : (j + 1) * 128] for j in range(4)], axis=0)
        else:
            out_ref[g] = best


def nearest_codes(codes, queries, best=None):
    shape = (8, 8, 512) if best is None else (8, 4, 128)
    operands = (codes, queries) if best is None else (codes, queries, best)
    return pl.pallas_call(
        nearest_kernel,
        out_shape=jax.ShapeDtypeStruct(shape, f32),
        compiler_params=pltpu.CompilerParams(vmem_limit_bytes=32 << 20),
        cost_estimate=pl.CostEstimate(flops=2 << 30, bytes_accessed=4 << 20, transcendentals=0),
        name="nearest",
    )(*operands)


def swap_cores(x):
    return lax.ppermute(x, "core", [(0, 1), (1, 0)])


def body(latents, batch_order, code_block, code_offset, ema_counts, ema_sums, queries):
    core = lax.axis_index("core").astype(i32)
    own = jnp.sum(jnp.square(queries.astype(f32)), axis=1)
    rows, mine = build(
        core.reshape(1),
        latents,
        batch_order,
        code_block.reshape(1, -1),
        code_offset.reshape(1, -1),
        queries,
    )
    pieces, at = [], 0
    for count in PIECES:
        pieces.append(lax.all_gather(mine[at : at + count], ("xa", "y"), axis=0, tiled=True))
        at += count
    plane_queries = stage(pieces)
    got = lax.all_to_all(rows.reshape(256, 9, 2, 128), ("zh", "xa", "xb", "y", "zl"), 0, 0, tiled=True)
    got = got.reshape(256 * 18, 128)
    arrived = plane_queries[:16]
    other_part = swap_cores(partial_update(1, got, arrived))
    own_part = partial_update(0, got, arrived)
    codebook, counts, sums, rounded = merge(own_part, other_part, ema_counts, ema_sums)
    far = lax.ppermute(rounded, ("zh", "zl"), [(z, 15 - z) for z in range(16)])
    near = lax.all_gather(rounded, ("xb", "core"), axis=0, tiled=True)
    best = nearest_codes(near, plane_queries)
    far = lax.all_gather(far, ("xb", "core"), axis=0, tiled=True)
    best = nearest_codes(far, plane_queries, best)
    found = jnp.min(lax.all_to_all(best, ("xa", "y"), 0, 0, tiled=True), axis=0)
    found = jnp.broadcast_to(found[None], (16, 4, 128))
    found = lax.all_to_all(found, ("zl", "core"), 0, 0, tiled=True)
    found = jnp.min(found.reshape(8, 2, 4, 128), axis=0).reshape(-1)
    nearest = (own + found) / E
    return (codebook, counts.reshape(-1), sums, nearest)


def solution(mesh):
    fine = Mesh(mesh.devices.reshape(SIZES), AXES)
    placed = (
        P(AXES, None),
        P(AXES, None),
        P(AXES, None),
        P(AXES),
        P(AXES),
        P(AXES, None),
        P(("zh", "xa", "xb", "y"), None),
    )
    return jax.shard_map(
        body,
        mesh=fine,
        in_specs=placed,
        out_specs=(P(AXES, None), P(AXES), P(AXES, None), P(("zh", "xa", "xb", "y"))),
        check_vma=False,
    )
```

```python
import functools

import jax
import jax.numpy as jnp
from jax import lax
from jax.experimental import pallas as pl
from jax.experimental.pallas import tpu as pltpu
from jax.sharding import Mesh, PartitionSpec as P

E = 256
CPD = 256
STEPS = 2
CAP = 2
SLOTS = STEPS * CAP
ema_decay = 0.9

AXES = ("zh", "x", "y", "zl", "core")
SIZES = (2, 4, 4, 8, 2)
NT = (((1,), (1,)), ((), ()))

f32 = jnp.float32
bf16 = jnp.bfloat16
i32 = jnp.int32


def iota(shape, dim):
    return lax.broadcasted_iota(i32, shape, dim)


def one_hot(hit):
    return jnp.where(hit, 1.0, 0.0).astype(bf16)


def build_kernel(core_ref, latents_hbm, order_hbm, block_hbm, offset_hbm, queries_hbm,
                 rows_ref, half_hbm, half_ref, latents_ref, order_ref,
                 block_ref, offset_ref, sems):
    tokens = latents_ref.shape[0]
    step = tokens // STEPS
    copies = [
        pltpu.make_async_copy(block_hbm, block_ref, sems.at[0]),
        pltpu.make_async_copy(offset_hbm, offset_ref, sems.at[1]),
        pltpu.make_async_copy(order_hbm, order_ref, sems.at[2]),
        pltpu.make_async_copy(latents_hbm, latents_ref, sems.at[3]),
    ]
    for copy in copies:
        copy.start()
    half = half_hbm.shape[0]
    side = pl.multiple_of(core_ref[0] * half, half)
    half_in = pltpu.make_async_copy(queries_hbm.at[pl.ds(side, half)], half_ref, sems.at[4])
    half_in.start()
    copies[0].wait()
    block = block_ref[...] ^ core_ref[0]
    earlier = one_hot(iota((step, step), 0) < iota((step, step), 1))
    ranks = []
    for t in range(STEPS):
        own = iota((512, step), 0) == block[:, t * step : (t + 1) * step]
        counts = jnp.dot(one_hot(own), earlier, preferred_element_type=f32)
        ranks.append(jnp.sum(jnp.where(own, counts, 0.0), axis=0, keepdims=True))
    rank = jnp.concatenate(ranks, axis=1).astype(i32)
    position = iota((1, tokens), 1)
    slot = jnp.where(position >= step, CAP, 0) + rank
    place = block * SLOTS + slot
    copies[1].wait()
    code = (offset_ref[...] + 1).astype(f32)
    lanes = jnp.where((iota((128, tokens), 0) & 7) == (place & 7), code, 0.0).astype(bf16)
    named = one_hot((iota((512, tokens), 0) >> 1) == (block >> 1))
    labels = lax.dot_general(named, lanes, NT, preferred_element_type=f32)
    labels = jnp.where((iota((512, 128), 0) & 1) == 1, pltpu.roll(labels, 4, 1), labels)
    labels = labels.reshape(64, 8, 128)
    half_in.wait()
    half_out = pltpu.make_async_copy(half_ref, half_hbm, sems.at[5])
    half_out.start()
    digits = jnp.where(iota((8, tokens), 0) == 0, place >> 6, place & 63).astype(f32).astype(bf16)
    copies[2].wait()
    stored = one_hot(iota((tokens, tokens), 0) == order_ref[...])
    pair = lax.dot_general(digits, stored, NT, preferred_element_type=f32).astype(i32)
    place = pair[0:1] * 64 + pair[1:2]
    copies[3].wait()
    latents = latents_ref[...]
    chunk = 512
    low = iota((chunk // 8, 8, 128), 1) < 4
    groups = chunk // 32
    row = iota((groups, 8, 128), 1)
    for c in range(512 * SLOTS // chunk):
        pick = one_hot(iota((chunk, tokens), 0) + c * chunk == place)
        got = jnp.dot(pick, latents, preferred_element_type=f32)
        a = got[:, :128].reshape(chunk // 8, 8, 128)
        b = got[:, 128:].reshape(chunk // 8, 8, 128)
        first = jnp.where(low, a, pltpu.roll(b, 4, 1))
        second = jnp.where(low, pltpu.roll(a, 4, 1), b)
        m = jnp.stack([first, second], axis=1).reshape(groups, 4, 2, 8, 128)
        label = labels[c * groups : (c + 1) * groups]
        a1, b1 = pltpu.roll(m[:, 1, 0], 2, 1), pltpu.roll(m[:, 1, 1], 2, 1)
        a2, b2 = pltpu.roll(m[:, 2, 0], 4, 1), pltpu.roll(m[:, 2, 1], 4, 1)
        a3, b3 = pltpu.roll(m[:, 3, 0], 6, 1), pltpu.roll(m[:, 3, 1], 6, 1)
        tiles = [
            m[:, 0, 0],
            m[:, 0, 1],
            jnp.where(row < 2, label, a1),
            jnp.where(row < 2, a1, b1),
            jnp.where(row < 2, b1, jnp.where(row < 4, label, a2)),
            jnp.where(row < 4, a2, b2),
            jnp.where(row < 4, b2, jnp.where(row < 6, label, a3)),
            jnp.where(row < 6, a3, b3),
            jnp.where(row < 6, b3, label),
        ]
        count = groups * 72
        rows_ref[c * count : (c + 1) * count] = (
            jnp.stack(tiles, axis=1).reshape(count, 128).astype(bf16)
        )
    half_out.wait()


def build(core, latents, order, block, offset, queries):
    return pl.pallas_call(
        build_kernel,
        out_shape=(
            jax.ShapeDtypeStruct((256 * 18, 128), bf16),
            jax.ShapeDtypeStruct((512, E), bf16),
        ),
        in_specs=[pl.BlockSpec(memory_space=pltpu.SMEM)] + [pl.BlockSpec(memory_space=pltpu.HBM)] * 5,
        out_specs=(
            pl.BlockSpec(memory_space=pltpu.VMEM),
            pl.BlockSpec(memory_space=pltpu.HBM),
        ),
        scratch_shapes=[
            pltpu.VMEM((512, E), bf16),
            pltpu.VMEM((1024, E), bf16),
            pltpu.VMEM((1, 1024), i32),
            pltpu.VMEM((1, 1024), i32),
            pltpu.VMEM((1, 1024), i32),
            pltpu.SemaphoreType.DMA((6,)),
        ],
        compiler_params=pltpu.CompilerParams(vmem_limit_bytes=60 << 20),
        cost_estimate=pl.CostEstimate(flops=3 << 30, bytes_accessed=2 << 20, transcendentals=0),
        name="build",
    )(core, latents, order, block, offset, queries)


def partial_kernel(side, rows_ref, queries_ref, out_ref, hit_ref):
    del queries_ref
    tiles = rows_ref[...].astype(f32).reshape(64, 9, 8, 128)
    row = iota((64, 8, 128), 1)
    label = jnp.where(row < 6, tiles[:, 6], tiles[:, 8])
    label = jnp.where(row < 2, tiles[:, 2], jnp.where(row < 4, tiles[:, 4], label))
    line, lane = iota((64, 128), 0), iota((64, 128), 1)
    keep = line == 2 * (lane >> 2) + (((lane >> 2) & 1) ^ side)
    code = jnp.sum(jnp.where(keep, label.reshape(8, 64, 128), 0.0), axis=1).astype(i32)
    local = iota((2 * CPD, 128), 0)
    step = ((iota((2 * CPD, 128), 1) & 3) >> 1) == (local >> 8)
    local = jnp.where(step, (local & 255) + 1, -1)
    for i in range(8):
        hit_ref[:, i * 128 : (i + 1) * 128] = one_hot(local == code[i : i + 1])
    messages = []
    for i in range(4):
        at, shift = (18 * i + 8 * side) // 8, (18 * i) % 8
        if shift:
            low = pltpu.roll(tiles[:, at], 8 - shift, 1)
            high = pltpu.roll(tiles[:, at + 1], 8 - shift, 1)
            messages.append(jnp.where(row < 8 - shift, low, high))
        else:
            messages.append(tiles[:, at])
    first = jnp.stack(messages[0::2], axis=1).reshape(128, 8, 128)
    second = jnp.stack(messages[1::2], axis=1).reshape(128, 8, 128)
    low = iota((128, 8, 128), 1) < 4
    left = jnp.where(low, first, pltpu.roll(second, 4, 1)).reshape(1024, 128)
    right = jnp.where(low, pltpu.roll(first, 4, 1), second).reshape(1024, 128)
    rows = jnp.concatenate([left, right], axis=1).astype(bf16)
    hits = hit_ref[...]
    sums = jnp.dot(hits, rows, preferred_element_type=f32)
    counts = lax.dot_general(jnp.ones((8, 1024), bf16), hits, NT, preferred_element_type=f32)
    keep_rate, add_rate = ema_decay, 1.0 - ema_decay
    out_ref[:CPD] = keep_rate * (add_rate * sums[:CPD]) + add_rate * sums[CPD:]
    out_ref[CPD:] = keep_rate * (add_rate * counts[:, :CPD]) + add_rate * counts[:, CPD:]


def partial_update(side, rows, queries):
    return pl.pallas_call(
        functools.partial(partial_kernel, side),
        out_shape=jax.ShapeDtypeStruct((CPD + 8, E), f32),
        in_specs=[pl.BlockSpec(memory_space=pltpu.VMEM), pl.BlockSpec(memory_space=pl.ANY)],
        scratch_shapes=[pltpu.VMEM((2 * CPD, 1024), bf16)],
        compiler_params=pltpu.CompilerParams(vmem_limit_bytes=32 << 20),
        cost_estimate=pl.CostEstimate(flops=1 << 29, bytes_accessed=2 << 20, transcendentals=0),
        name="partial",
    )(rows, queries)


def merge_kernel(own_ref, other_ref, counts_ref, sums_ref, codebook_ref, new_counts_ref, new_sums_ref, rounded_ref):
    rows = own_ref[CPD:] + other_ref[CPD:]
    rows = ema_decay * (ema_decay * counts_ref[...]) + rows
    sums = ema_decay * (ema_decay * sums_ref[...]) + (own_ref[:CPD] + other_ref[:CPD])
    cols = jnp.transpose(jnp.broadcast_to(rows[0:1], (128, CPD)))
    book = jnp.concatenate([sums[:, :128] / cols, sums[:, 128:] / cols], axis=1)
    codebook_ref[...] = book
    rounded_ref[...] = book.astype(bf16)
    new_sums_ref[...] = sums
    new_counts_ref[...] = rows[0:1]


def merge(own, other, counts, sums):
    return pl.pallas_call(
        merge_kernel,
        out_shape=(
            jax.ShapeDtypeStruct((CPD, E), f32),
            jax.ShapeDtypeStruct((1, CPD), f32),
            jax.ShapeDtypeStruct((CPD, E), f32),
            jax.ShapeDtypeStruct((CPD, E), bf16),
        ),
        compiler_params=pltpu.CompilerParams(vmem_limit_bytes=32 << 20),
        cost_estimate=pl.CostEstimate(flops=1 << 20, bytes_accessed=2 << 20, transcendentals=0),
        name="merge",
    )(own, other, counts.reshape(1, CPD), sums)


def nearest_kernel(codes_ref, low_ref, high_ref, *refs):
    out_ref = refs[-1]
    last = out_ref.shape == (32, 4, 128)
    scaled, norms = [], []
    for c in range(codes_ref.shape[0] // CPD):
        part = codes_ref[c * CPD : (c + 1) * CPD].astype(f32)
        norms.append(jnp.sum(part * part, axis=1, keepdims=True))
        scaled.append((-2.0 * part).astype(bf16))
    for y in range(4):
        lines = []
        for h, queries_ref in enumerate((low_ref, high_ref)):
            part = queries_ref[y * 256 : (y + 1) * 256]
            best = refs[0][2 * y + h] if len(refs) > 1 else None
            for m, n in zip(scaled, norms):
                value = lax.dot_general(m, part, NT, preferred_element_type=f32) + n
                value = jnp.min(value.reshape(CPD // 8, 8, 256), axis=0)
                best = value if best is None else jnp.minimum(best, value)
            if last:
                line = jnp.min(best, axis=0, keepdims=True)
                lines += [line[:, :128], line[:, 128:]]
            else:
                out_ref[2 * y + h] = best
        if last:
            lines = jnp.concatenate(lines, axis=0)
            for z in range(8):
                out_ref[y * 8 + z] = lines


def nearest_codes(codes, queries, best=None, last=False):
    shape = (32, 4, 128) if last else (8, 8, 256)
    operands = (codes, *queries) if best is None else (codes, *queries, best)
    return pl.pallas_call(
        nearest_kernel,
        out_shape=jax.ShapeDtypeStruct(shape, f32),
        compiler_params=pltpu.CompilerParams(vmem_limit_bytes=32 << 20),
        cost_estimate=pl.CostEstimate(flops=1 << 30, bytes_accessed=2 << 20, transcendentals=0),
        name="nearest",
    )(*operands)


def swap_cores(x):
    return lax.ppermute(x, "core", [(0, 1), (1, 0)])


def body(latents, batch_order, code_block, code_offset, ema_counts, ema_sums, queries):
    core = lax.axis_index("core").astype(i32)
    own = jnp.sum(jnp.square(queries.astype(f32)), axis=1)
    rows, mine = build(
        core.reshape(1),
        latents,
        batch_order,
        code_block.reshape(1, -1),
        code_offset.reshape(1, -1),
        queries,
    )
    row_queries = [
        lax.all_gather(part, "y", axis=0, tiled=True) for part in (mine[:256], mine[256:])
    ]
    got = lax.all_to_all(rows.reshape(256, 9, 2, 128), ("zh", "x", "y", "zl"), 0, 0, tiled=True)
    got = got.reshape(256 * 18, 128)
    arrived = row_queries[0][:16] + row_queries[1][:16]
    other_part = swap_cores(partial_update(1, got, arrived))
    own_part = partial_update(0, got, arrived)
    codebook, counts, sums, rounded = merge(own_part, other_part, ema_counts, ema_sums)
    far = lax.ppermute(rounded, ("zh", "zl"), [(z, 15 - z) for z in range(16)])
    near = lax.all_gather(rounded, "x", axis=0, tiled=True)
    near_other = swap_cores(near)
    best = nearest_codes(near, row_queries)
    best = nearest_codes(near_other, row_queries, best)
    far = lax.all_gather(far, "x", axis=0, tiled=True)
    far_other = swap_cores(far)
    best = nearest_codes(far, row_queries, best)
    best = nearest_codes(far_other, row_queries, best, last=True)
    found = jnp.min(lax.all_to_all(best, ("y", "zl"), 0, 0, tiled=True), axis=0)
    found = lax.all_gather(found, "core", axis=0, tiled=True).reshape(-1)
    nearest = (own + found) / E
    return (codebook, counts.reshape(-1), sums, nearest)


def solution(mesh):
    fine = Mesh(mesh.devices.reshape(SIZES), AXES)
    placed = (
        P(AXES, None),
        P(AXES, None),
        P(AXES, None),
        P(AXES),
        P(AXES),
        P(AXES, None),
        P(("zh", "x", "y"), None),
    )
    return jax.shard_map(
        body,
        mesh=fine,
        in_specs=placed,
        out_specs=(P(AXES, None), P(AXES), P(AXES, None), P(("zh", "x", "y"))),
        check_vma=False,
    )
```

```python
import functools

import jax
import jax.numpy as jnp
from jax import lax
from jax.experimental import pallas as pl
from jax.experimental.pallas import tpu as pltpu
from jax.sharding import Mesh, PartitionSpec as P

E = 256
CPD = 256
STEPS = 2
CAP = 2
SLOTS = STEPS * CAP
ema_decay = 0.9

AXES = ("zh", "xa", "xb", "y", "zl", "core")
SIZES = (2, 2, 2, 4, 8, 2)
NT = (((1,), (1,)), ((), ()))

f32 = jnp.float32
bf16 = jnp.bfloat16
i32 = jnp.int32


def iota(shape, dim):
    return lax.broadcasted_iota(i32, shape, dim)


def one_hot(hit):
    return jnp.where(hit, 1.0, 0.0).astype(bf16)


def build_kernel(core_ref, latents_hbm, order_hbm, block_hbm, offset_hbm, queries_hbm,
                 rows_ref, half_hbm, half_ref, latents_ref, order_ref,
                 block_ref, offset_ref, sems):
    tokens = latents_ref.shape[0]
    step = tokens // STEPS
    copies = [
        pltpu.make_async_copy(block_hbm, block_ref, sems.at[0]),
        pltpu.make_async_copy(offset_hbm, offset_ref, sems.at[1]),
        pltpu.make_async_copy(order_hbm, order_ref, sems.at[2]),
        pltpu.make_async_copy(latents_hbm, latents_ref, sems.at[3]),
    ]
    for copy in copies:
        copy.start()
    half = half_hbm.shape[0]
    side = pl.multiple_of(core_ref[0] * half, half)
    half_in = pltpu.make_async_copy(queries_hbm.at[pl.ds(side, half)], half_ref, sems.at[4])
    half_in.start()
    copies[0].wait()
    block = block_ref[...] ^ core_ref[0]
    earlier = one_hot(iota((step, step), 0) < iota((step, step), 1))
    ranks = []
    for t in range(STEPS):
        own = iota((512, step), 0) == block[:, t * step : (t + 1) * step]
        counts = jnp.dot(one_hot(own), earlier, preferred_element_type=f32)
        ranks.append(jnp.sum(jnp.where(own, counts, 0.0), axis=0, keepdims=True))
    rank = jnp.concatenate(ranks, axis=1).astype(i32)
    position = iota((1, tokens), 1)
    slot = jnp.where(position >= step, CAP, 0) + rank
    place = block * SLOTS + slot
    copies[1].wait()
    code = (offset_ref[...] + 1).astype(f32)
    lanes = jnp.where((iota((128, tokens), 0) & 7) == (place & 7), code, 0.0).astype(bf16)
    named = one_hot((iota((512, tokens), 0) >> 1) == (block >> 1))
    labels = lax.dot_general(named, lanes, NT, preferred_element_type=f32)
    labels = jnp.where((iota((512, 128), 0) & 1) == 1, pltpu.roll(labels, 4, 1), labels)
    labels = labels.reshape(64, 8, 128)
    half_in.wait()
    half_out = pltpu.make_async_copy(half_ref, half_hbm, sems.at[5])
    half_out.start()
    digits = jnp.where(iota((8, tokens), 0) == 0, place >> 6, place & 63).astype(f32).astype(bf16)
    copies[2].wait()
    stored = one_hot(iota((tokens, tokens), 0) == order_ref[...])
    pair = lax.dot_general(digits, stored, NT, preferred_element_type=f32).astype(i32)
    place = pair[0:1] * 64 + pair[1:2]
    copies[3].wait()
    latents = latents_ref[...]
    chunk = 512
    low = iota((chunk // 8, 8, 128), 1) < 4
    groups = chunk // 32
    row = iota((groups, 8, 128), 1)
    for c in range(512 * SLOTS // chunk):
        pick = one_hot(iota((chunk, tokens), 0) + c * chunk == place)
        got = jnp.dot(pick, latents, preferred_element_type=f32)
        a = got[:, :128].reshape(chunk // 8, 8, 128)
        b = got[:, 128:].reshape(chunk // 8, 8, 128)
        first = jnp.where(low, a, pltpu.roll(b, 4, 1))
        second = jnp.where(low, pltpu.roll(a, 4, 1), b)
        m = jnp.stack([first, second], axis=1).reshape(groups, 4, 2, 8, 128)
        label = labels[c * groups : (c + 1) * groups]
        a1, b1 = pltpu.roll(m[:, 1, 0], 2, 1), pltpu.roll(m[:, 1, 1], 2, 1)
        a2, b2 = pltpu.roll(m[:, 2, 0], 4, 1), pltpu.roll(m[:, 2, 1], 4, 1)
        a3, b3 = pltpu.roll(m[:, 3, 0], 6, 1), pltpu.roll(m[:, 3, 1], 6, 1)
        tiles = [
            m[:, 0, 0],
            m[:, 0, 1],
            jnp.where(row < 2, label, a1),
            jnp.where(row < 2, a1, b1),
            jnp.where(row < 2, b1, jnp.where(row < 4, label, a2)),
            jnp.where(row < 4, a2, b2),
            jnp.where(row < 4, b2, jnp.where(row < 6, label, a3)),
            jnp.where(row < 6, a3, b3),
            jnp.where(row < 6, b3, label),
        ]
        count = groups * 72
        rows_ref[c * count : (c + 1) * count] = (
            jnp.stack(tiles, axis=1).reshape(count, 128).astype(bf16)
        )
    half_out.wait()


def build(core, latents, order, block, offset, queries):
    return pl.pallas_call(
        build_kernel,
        out_shape=(
            jax.ShapeDtypeStruct((256 * 18, 128), bf16),
            jax.ShapeDtypeStruct((512, E), bf16),
        ),
        in_specs=[pl.BlockSpec(memory_space=pltpu.SMEM)] + [pl.BlockSpec(memory_space=pltpu.HBM)] * 5,
        out_specs=(
            pl.BlockSpec(memory_space=pltpu.VMEM),
            pl.BlockSpec(memory_space=pltpu.HBM),
        ),
        scratch_shapes=[
            pltpu.VMEM((512, E), bf16),
            pltpu.VMEM((1024, E), bf16),
            pltpu.VMEM((1, 1024), i32),
            pltpu.VMEM((1, 1024), i32),
            pltpu.VMEM((1, 1024), i32),
            pltpu.SemaphoreType.DMA((6,)),
        ],
        compiler_params=pltpu.CompilerParams(vmem_limit_bytes=60 << 20),
        cost_estimate=pl.CostEstimate(flops=3 << 30, bytes_accessed=2 << 20, transcendentals=0),
        name="build",
    )(core, latents, order, block, offset, queries)


def partial_kernel(side, rows_ref, queries_ref, out_ref, hit_ref):
    del queries_ref
    tiles = rows_ref[...].astype(f32).reshape(64, 9, 8, 128)
    row = iota((64, 8, 128), 1)
    label = jnp.where(row < 6, tiles[:, 6], tiles[:, 8])
    label = jnp.where(row < 2, tiles[:, 2], jnp.where(row < 4, tiles[:, 4], label))
    line, lane = iota((64, 128), 0), iota((64, 128), 1)
    keep = line == 2 * (lane >> 2) + (((lane >> 2) & 1) ^ side)
    code = jnp.sum(jnp.where(keep, label.reshape(8, 64, 128), 0.0), axis=1).astype(i32)
    local = iota((2 * CPD, 128), 0)
    step = ((iota((2 * CPD, 128), 1) & 3) >> 1) == (local >> 8)
    local = jnp.where(step, (local & 255) + 1, -1)
    for i in range(8):
        hit_ref[:, i * 128 : (i + 1) * 128] = one_hot(local == code[i : i + 1])
    messages = []
    for i in range(4):
        at, shift = (18 * i + 8 * side) // 8, (18 * i) % 8
        if shift:
            low = pltpu.roll(tiles[:, at], 8 - shift, 1)
            high = pltpu.roll(tiles[:, at + 1], 8 - shift, 1)
            messages.append(jnp.where(row < 8 - shift, low, high))
        else:
            messages.append(tiles[:, at])
    first = jnp.stack(messages[0::2], axis=1).reshape(128, 8, 128)
    second = jnp.stack(messages[1::2], axis=1).reshape(128, 8, 128)
    low = iota((128, 8, 128), 1) < 4
    left = jnp.where(low, first, pltpu.roll(second, 4, 1)).reshape(1024, 128)
    right = jnp.where(low, pltpu.roll(first, 4, 1), second).reshape(1024, 128)
    rows = jnp.concatenate([left, right], axis=1).astype(bf16)
    hits = hit_ref[...]
    sums = jnp.dot(hits, rows, preferred_element_type=f32)
    counts = lax.dot_general(jnp.ones((8, 1024), bf16), hits, NT, preferred_element_type=f32)
    keep_rate, add_rate = ema_decay, 1.0 - ema_decay
    out_ref[:CPD] = keep_rate * (add_rate * sums[:CPD]) + add_rate * sums[CPD:]
    out_ref[CPD:] = keep_rate * (add_rate * counts[:, :CPD]) + add_rate * counts[:, CPD:]


def partial_update(side, rows, queries):
    return pl.pallas_call(
        functools.partial(partial_kernel, side),
        out_shape=jax.ShapeDtypeStruct((CPD + 8, E), f32),
        in_specs=[pl.BlockSpec(memory_space=pltpu.VMEM), pl.BlockSpec(memory_space=pl.ANY)],
        scratch_shapes=[pltpu.VMEM((2 * CPD, 1024), bf16)],
        compiler_params=pltpu.CompilerParams(vmem_limit_bytes=32 << 20),
        cost_estimate=pl.CostEstimate(flops=1 << 29, bytes_accessed=2 << 20, transcendentals=0),
        name="partial",
    )(rows, queries)


def merge_kernel(own_ref, other_ref, counts_ref, sums_ref, codebook_ref, new_counts_ref, new_sums_ref, rounded_ref):
    rows = own_ref[CPD:] + other_ref[CPD:]
    rows = ema_decay * (ema_decay * counts_ref[...]) + rows
    sums = ema_decay * (ema_decay * sums_ref[...]) + (own_ref[:CPD] + other_ref[:CPD])
    cols = jnp.transpose(jnp.broadcast_to(rows[0:1], (128, CPD)))
    book = jnp.concatenate([sums[:, :128] / cols, sums[:, 128:] / cols], axis=1)
    codebook_ref[...] = book
    rounded_ref[...] = book.astype(bf16)
    new_sums_ref[...] = sums
    new_counts_ref[...] = rows[0:1]


def merge(own, other, counts, sums):
    return pl.pallas_call(
        merge_kernel,
        out_shape=(
            jax.ShapeDtypeStruct((CPD, E), f32),
            jax.ShapeDtypeStruct((1, CPD), f32),
            jax.ShapeDtypeStruct((CPD, E), f32),
            jax.ShapeDtypeStruct((CPD, E), bf16),
        ),
        compiler_params=pltpu.CompilerParams(vmem_limit_bytes=32 << 20),
        cost_estimate=pl.CostEstimate(flops=1 << 20, bytes_accessed=2 << 20, transcendentals=0),
        name="merge",
    )(own, other, counts.reshape(1, CPD), sums)


def nearest_kernel(side_ref, codes_ref, *refs):
    queries_refs, out_ref = refs[:4], refs[-1]
    last = out_ref.shape == (64, 4, 128)
    scaled, norms = [], []
    for c in range(codes_ref.shape[0] // CPD):
        part = codes_ref[c * CPD : (c + 1) * CPD].astype(f32)
        norms.append(jnp.sum(part * part, axis=1, keepdims=True))
        scaled.append((-2.0 * part).astype(bf16))
    for g in range(8):
        other, y = g // 4, g % 4
        lines = []
        for h in range(2):
            part = queries_refs[2 * other + h][y * 256 : (y + 1) * 256]
            best = refs[4][2 * g + h] if last else None
            for m, n in zip(scaled, norms):
                value = lax.dot_general(m, part, NT, preferred_element_type=f32) + n
                value = jnp.min(value.reshape(CPD // 8, 8, 256), axis=0)
                best = value if best is None else jnp.minimum(best, value)
            if last:
                line = jnp.min(best, axis=0, keepdims=True)
                lines += [line[:, :128], line[:, 128:]]
            else:
                out_ref[2 * g + h] = best
        if last:
            lines = jnp.concatenate(lines, axis=0)
            at = (side_ref[0] ^ other) * 32 + y * 8
            for z in range(8):
                out_ref[at + z] = lines


def nearest_codes(side, codes, queries, best=None):
    shape = (16, 8, 256) if best is None else (64, 4, 128)
    operands = (side, codes, *queries) if best is None else (side, codes, *queries, best)
    vmem = pl.BlockSpec(memory_space=pltpu.VMEM)
    return pl.pallas_call(
        nearest_kernel,
        out_shape=jax.ShapeDtypeStruct(shape, f32),
        in_specs=[pl.BlockSpec(memory_space=pltpu.SMEM)] + [vmem] * (len(operands) - 1),
        out_specs=vmem,
        compiler_params=pltpu.CompilerParams(vmem_limit_bytes=32 << 20),
        cost_estimate=pl.CostEstimate(flops=2 << 30, bytes_accessed=4 << 20, transcendentals=0),
        name="nearest",
    )(*operands)


def swap_cores(x):
    return lax.ppermute(x, "core", [(0, 1), (1, 0)])


def body(latents, batch_order, code_block, code_offset, ema_counts, ema_sums, queries):
    core = lax.axis_index("core").astype(i32)
    own = jnp.sum(jnp.square(queries.astype(f32)), axis=1)
    rows, mine = build(
        core.reshape(1),
        latents,
        batch_order,
        code_block.reshape(1, -1),
        code_offset.reshape(1, -1),
        queries,
    )
    across = lax.ppermute(mine, "xa", [(0, 1), (1, 0)])
    row_queries = [
        lax.all_gather(part, "y", axis=0, tiled=True)
        for part in (mine[:256], mine[256:], across[:256], across[256:])
    ]
    side = lax.axis_index("xa").astype(i32).reshape(1)
    got = lax.all_to_all(rows.reshape(256, 9, 2, 128), ("zh", "xa", "xb", "y", "zl"), 0, 0, tiled=True)
    got = got.reshape(256 * 18, 128)
    arrived = (row_queries[0][:16] + row_queries[1][:16]) + (row_queries[2][:16] + row_queries[3][:16])
    other_part = swap_cores(partial_update(1, got, arrived))
    own_part = partial_update(0, got, arrived)
    codebook, counts, sums, rounded = merge(own_part, other_part, ema_counts, ema_sums)
    far = lax.ppermute(rounded, ("zh", "zl"), [(z, 15 - z) for z in range(16)])
    near = lax.all_gather(rounded, ("xb", "core"), axis=0, tiled=True)
    best = nearest_codes(side, near, row_queries)
    far = lax.all_gather(far, ("xb", "core"), axis=0, tiled=True)
    best = nearest_codes(side, far, row_queries, best)
    found = jnp.min(lax.all_to_all(best, ("xa", "y", "zl"), 0, 0, tiled=True), axis=0)
    found = lax.all_gather(found, "core", axis=0, tiled=True).reshape(-1)
    nearest = (own + found) / E
    return (codebook, counts.reshape(-1), sums, nearest)


def solution(mesh):
    fine = Mesh(mesh.devices.reshape(SIZES), AXES)
    placed = (
        P(AXES, None),
        P(AXES, None),
        P(AXES, None),
        P(AXES),
        P(AXES),
        P(AXES, None),
        P(("zh", "xa", "xb", "y"), None),
    )
    return jax.shard_map(
        body,
        mesh=fine,
        in_specs=placed,
        out_specs=(P(AXES, None), P(AXES), P(AXES, None), P(("zh", "xa", "xb", "y"))),
        check_vma=False,
    )
```

```python
import functools

import jax
import jax.numpy as jnp
from jax import lax
from jax.experimental import pallas as pl
from jax.experimental.pallas import tpu as pltpu
from jax.sharding import Mesh, PartitionSpec as P

E = 256
CPD = 256
STEPS = 2
CAP = 2
SLOTS = STEPS * CAP
ema_decay = 0.9

AXES = ("zh", "xa", "xb", "y", "zl", "core")
SIZES = (2, 2, 2, 4, 8, 2)
NT = (((1,), (1,)), ((), ()))

f32 = jnp.float32
bf16 = jnp.bfloat16
i32 = jnp.int32


def iota(shape, dim):
    return lax.broadcasted_iota(i32, shape, dim)


def one_hot(hit):
    return jnp.where(hit, 1.0, 0.0).astype(bf16)


def build_kernel(core_ref, latents_hbm, order_hbm, block_hbm, offset_hbm, queries_hbm,
                 rows_ref, half_hbm, half_ref, latents_ref, order_ref,
                 block_ref, offset_ref, sems):
    tokens = latents_ref.shape[0]
    step = tokens // STEPS
    copies = [
        pltpu.make_async_copy(block_hbm, block_ref, sems.at[0]),
        pltpu.make_async_copy(offset_hbm, offset_ref, sems.at[1]),
        pltpu.make_async_copy(order_hbm, order_ref, sems.at[2]),
        pltpu.make_async_copy(latents_hbm, latents_ref, sems.at[3]),
    ]
    for copy in copies:
        copy.start()
    half = half_hbm.shape[0]
    side = pl.multiple_of(core_ref[0] * half, half)
    half_in = pltpu.make_async_copy(queries_hbm.at[pl.ds(side, half)], half_ref, sems.at[4])
    half_in.start()
    copies[0].wait()
    block = block_ref[...] ^ core_ref[0]
    earlier = one_hot(iota((step, step), 0) < iota((step, step), 1))
    ranks = []
    for t in range(STEPS):
        own = iota((512, step), 0) == block[:, t * step : (t + 1) * step]
        counts = jnp.dot(one_hot(own), earlier, preferred_element_type=f32)
        ranks.append(jnp.sum(jnp.where(own, counts, 0.0), axis=0, keepdims=True))
    rank = jnp.concatenate(ranks, axis=1).astype(i32)
    position = iota((1, tokens), 1)
    slot = jnp.where(position >= step, CAP, 0) + rank
    place = block * SLOTS + slot
    copies[1].wait()
    code = (offset_ref[...] + 1).astype(f32)
    lanes = jnp.where((iota((128, tokens), 0) & 7) == (place & 7), code, 0.0).astype(bf16)
    named = one_hot((iota((512, tokens), 0) >> 1) == (block >> 1))
    labels = lax.dot_general(named, lanes, NT, preferred_element_type=f32)
    labels = jnp.where((iota((512, 128), 0) & 1) == 1, pltpu.roll(labels, 4, 1), labels)
    labels = labels.reshape(64, 8, 128)
    half_in.wait()
    half_out = pltpu.make_async_copy(half_ref, half_hbm, sems.at[5])
    half_out.start()
    digits = jnp.where(iota((8, tokens), 0) == 0, place >> 6, place & 63).astype(f32).astype(bf16)
    copies[2].wait()
    stored = one_hot(iota((tokens, tokens), 0) == order_ref[...])
    pair = lax.dot_general(digits, stored, NT, preferred_element_type=f32).astype(i32)
    place = pair[0:1] * 64 + pair[1:2]
    copies[3].wait()
    latents = latents_ref[...]
    chunk = 512
    low = iota((chunk // 8, 8, 128), 1) < 4
    groups = chunk // 32
    row = iota((groups, 8, 128), 1)
    for c in range(512 * SLOTS // chunk):
        pick = one_hot(iota((chunk, tokens), 0) + c * chunk == place)
        got = jnp.dot(pick, latents, preferred_element_type=f32)
        a = got[:, :128].reshape(chunk // 8, 8, 128)
        b = got[:, 128:].reshape(chunk // 8, 8, 128)
        first = jnp.where(low, a, pltpu.roll(b, 4, 1))
        second = jnp.where(low, pltpu.roll(a, 4, 1), b)
        m = jnp.stack([first, second], axis=1).reshape(groups, 4, 2, 8, 128)
        label = labels[c * groups : (c + 1) * groups]
        a1, b1 = pltpu.roll(m[:, 1, 0], 2, 1), pltpu.roll(m[:, 1, 1], 2, 1)
        a2, b2 = pltpu.roll(m[:, 2, 0], 4, 1), pltpu.roll(m[:, 2, 1], 4, 1)
        a3, b3 = pltpu.roll(m[:, 3, 0], 6, 1), pltpu.roll(m[:, 3, 1], 6, 1)
        tiles = [
            m[:, 0, 0],
            m[:, 0, 1],
            jnp.where(row < 2, label, a1),
            jnp.where(row < 2, a1, b1),
            jnp.where(row < 2, b1, jnp.where(row < 4, label, a2)),
            jnp.where(row < 4, a2, b2),
            jnp.where(row < 4, b2, jnp.where(row < 6, label, a3)),
            jnp.where(row < 6, a3, b3),
            jnp.where(row < 6, b3, label),
        ]
        count = groups * 72
        rows_ref[c * count : (c + 1) * count] = (
            jnp.stack(tiles, axis=1).reshape(count, 128).astype(bf16)
        )
    half_out.wait()


def build(core, latents, order, block, offset, queries):
    return pl.pallas_call(
        build_kernel,
        out_shape=(
            jax.ShapeDtypeStruct((256 * 18, 128), bf16),
            jax.ShapeDtypeStruct((512, E), bf16),
        ),
        in_specs=[pl.BlockSpec(memory_space=pltpu.SMEM)] + [pl.BlockSpec(memory_space=pltpu.HBM)] * 5,
        out_specs=(
            pl.BlockSpec(memory_space=pltpu.VMEM),
            pl.BlockSpec(memory_space=pltpu.HBM),
        ),
        scratch_shapes=[
            pltpu.VMEM((512, E), bf16),
            pltpu.VMEM((1024, E), bf16),
            pltpu.VMEM((1, 1024), i32),
            pltpu.VMEM((1, 1024), i32),
            pltpu.VMEM((1, 1024), i32),
            pltpu.SemaphoreType.DMA((6,)),
        ],
        compiler_params=pltpu.CompilerParams(vmem_limit_bytes=60 << 20),
        cost_estimate=pl.CostEstimate(flops=3 << 30, bytes_accessed=2 << 20, transcendentals=0),
        name="build",
    )(core, latents, order, block, offset, queries)


def partial_kernel(side, rows_ref, queries_ref, out_ref, hit_ref):
    del queries_ref
    tiles = rows_ref[...].astype(f32).reshape(64, 9, 8, 128)
    row = iota((64, 8, 128), 1)
    label = jnp.where(row < 6, tiles[:, 6], tiles[:, 8])
    label = jnp.where(row < 2, tiles[:, 2], jnp.where(row < 4, tiles[:, 4], label))
    line, lane = iota((64, 128), 0), iota((64, 128), 1)
    keep = line == 2 * (lane >> 2) + (((lane >> 2) & 1) ^ side)
    code = jnp.sum(jnp.where(keep, label.reshape(8, 64, 128), 0.0), axis=1).astype(i32)
    local = iota((2 * CPD, 128), 0)
    step = ((iota((2 * CPD, 128), 1) & 3) >> 1) == (local >> 8)
    local = jnp.where(step, (local & 255) + 1, -1)
    for i in range(8):
        hit_ref[:, i * 128 : (i + 1) * 128] = one_hot(local == code[i : i + 1])
    messages = []
    for i in range(4):
        at, shift = (18 * i + 8 * side) // 8, (18 * i) % 8
        if shift:
            low = pltpu.roll(tiles[:, at], 8 - shift, 1)
            high = pltpu.roll(tiles[:, at + 1], 8 - shift, 1)
            messages.append(jnp.where(row < 8 - shift, low, high))
        else:
            messages.append(tiles[:, at])
    first = jnp.stack(messages[0::2], axis=1).reshape(128, 8, 128)
    second = jnp.stack(messages[1::2], axis=1).reshape(128, 8, 128)
    low = iota((128, 8, 128), 1) < 4
    left = jnp.where(low, first, pltpu.roll(second, 4, 1)).reshape(1024, 128)
    right = jnp.where(low, pltpu.roll(first, 4, 1), second).reshape(1024, 128)
    rows = jnp.concatenate([left, right], axis=1).astype(bf16)
    hits = hit_ref[...]
    sums = jnp.dot(hits, rows, preferred_element_type=f32)
    counts = lax.dot_general(jnp.ones((8, 1024), bf16), hits, NT, preferred_element_type=f32)
    keep_rate, add_rate = ema_decay, 1.0 - ema_decay
    out_ref[:CPD] = keep_rate * (add_rate * sums[:CPD]) + add_rate * sums[CPD:]
    out_ref[CPD:] = keep_rate * (add_rate * counts[:, :CPD]) + add_rate * counts[:, CPD:]


def partial_update(side, rows, queries):
    return pl.pallas_call(
        functools.partial(partial_kernel, side),
        out_shape=jax.ShapeDtypeStruct((CPD + 8, E), f32),
        in_specs=[pl.BlockSpec(memory_space=pltpu.VMEM), pl.BlockSpec(memory_space=pl.ANY)],
        scratch_shapes=[pltpu.VMEM((2 * CPD, 1024), bf16)],
        compiler_params=pltpu.CompilerParams(vmem_limit_bytes=32 << 20),
        cost_estimate=pl.CostEstimate(flops=1 << 29, bytes_accessed=2 << 20, transcendentals=0),
        name="partial",
    )(rows, queries)


def merge_kernel(own_ref, other_ref, counts_ref, sums_ref, codebook_ref, new_counts_ref, new_sums_ref, rounded_ref):
    rows = own_ref[CPD:] + other_ref[CPD:]
    rows = ema_decay * (ema_decay * counts_ref[...]) + rows
    sums = ema_decay * (ema_decay * sums_ref[...]) + (own_ref[:CPD] + other_ref[:CPD])
    cols = jnp.transpose(jnp.broadcast_to(rows[0:1], (128, CPD)))
    book = jnp.concatenate([sums[:, :128] / cols, sums[:, 128:] / cols], axis=1)
    codebook_ref[...] = book
    rounded_ref[...] = book.astype(bf16)
    new_sums_ref[...] = sums
    new_counts_ref[...] = rows[0:1]


def merge(own, other, counts, sums):
    return pl.pallas_call(
        merge_kernel,
        out_shape=(
            jax.ShapeDtypeStruct((CPD, E), f32),
            jax.ShapeDtypeStruct((1, CPD), f32),
            jax.ShapeDtypeStruct((CPD, E), f32),
            jax.ShapeDtypeStruct((CPD, E), bf16),
        ),
        compiler_params=pltpu.CompilerParams(vmem_limit_bytes=32 << 20),
        cost_estimate=pl.CostEstimate(flops=1 << 20, bytes_accessed=2 << 20, transcendentals=0),
        name="merge",
    )(own, other, counts.reshape(1, CPD), sums)


def nearest_kernel(codes_ref, low_ref, high_ref, *refs):
    out_ref = refs[-1]
    last = out_ref.shape == (4, 4, 128)
    scaled, norms = [], []
    for c in range(codes_ref.shape[0] // CPD):
        part = codes_ref[c * CPD : (c + 1) * CPD].astype(f32)
        norms.append(jnp.sum(part * part, axis=1, keepdims=True))
        scaled.append((-2.0 * part).astype(bf16))
    for y in range(4):
        lines = []
        for h, queries_ref in enumerate((low_ref, high_ref)):
            part = queries_ref[y * 256 : (y + 1) * 256]
            best = refs[0][2 * y + h] if len(refs) > 1 else None
            for m, n in zip(scaled, norms):
                value = lax.dot_general(m, part, NT, preferred_element_type=f32) + n
                value = jnp.min(value.reshape(CPD // 8, 8, 256), axis=0)
                best = value if best is None else jnp.minimum(best, value)
            if last:
                line = jnp.min(best, axis=0, keepdims=True)
                lines += [line[:, :128], line[:, 128:]]
            else:
                out_ref[2 * y + h] = best
        if last:
            out_ref[y] = jnp.concatenate(lines, axis=0)


def nearest_codes(codes, queries, best=None, last=False):
    shape = (4, 4, 128) if last else (8, 8, 256)
    operands = (codes, *queries) if best is None else (codes, *queries, best)
    return pl.pallas_call(
        nearest_kernel,
        out_shape=jax.ShapeDtypeStruct(shape, f32),
        compiler_params=pltpu.CompilerParams(vmem_limit_bytes=32 << 20),
        cost_estimate=pl.CostEstimate(flops=1 << 30, bytes_accessed=2 << 20, transcendentals=0),
        name="nearest",
    )(*operands)


def swap_cores(x):
    return lax.ppermute(x, "core", [(0, 1), (1, 0)])


def body(latents, batch_order, code_block, code_offset, ema_counts, ema_sums, queries):
    core = lax.axis_index("core").astype(i32)
    own = jnp.sum(jnp.square(queries.astype(f32)), axis=1)
    rows, mine = build(
        core.reshape(1),
        latents,
        batch_order,
        code_block.reshape(1, -1),
        code_offset.reshape(1, -1),
        queries,
    )
    across = lax.ppermute(mine, "xa", [(0, 1), (1, 0)])
    row_queries = [
        lax.all_gather(part, "y", axis=0, tiled=True)
        for part in (mine[:256], mine[256:], across[:256], across[256:])
    ]
    got = lax.all_to_all(rows.reshape(256, 9, 2, 128), ("zh", "xa", "xb", "y", "zl"), 0, 0, tiled=True)
    got = got.reshape(256 * 18, 128)
    arrived = (row_queries[0][:16] + row_queries[1][:16]) + (row_queries[2][:16] + row_queries[3][:16])
    other_part = swap_cores(partial_update(1, got, arrived))
    own_part = partial_update(0, got, arrived)
    codebook, counts, sums, rounded = merge(own_part, other_part, ema_counts, ema_sums)
    far = lax.ppermute(rounded, ("zh", "zl"), [(z, 15 - z) for z in range(16)])
    near = lax.all_gather(rounded, ("xb", "core"), axis=0, tiled=True)
    own_best = nearest_codes(near, row_queries[:2])
    across_best = nearest_codes(near, row_queries[2:])
    far = lax.all_gather(far, ("xb", "core"), axis=0, tiled=True)
    across_best = nearest_codes(far, row_queries[2:], across_best, last=True)
    returned = lax.ppermute(across_best, "xa", [(0, 1), (1, 0)])
    own_best = nearest_codes(far, row_queries[:2], own_best, last=True)
    best = jnp.minimum(own_best, returned)
    best = jnp.broadcast_to(best[:, None], (4, 8, 4, 128)).reshape(32, 4, 128)
    found = jnp.min(lax.all_to_all(best, ("y", "zl"), 0, 0, tiled=True), axis=0)
    found = lax.all_gather(found, "core", axis=0, tiled=True).reshape(-1)
    nearest = (own + found) / E
    return (codebook, counts.reshape(-1), sums, nearest)


def solution(mesh):
    fine = Mesh(mesh.devices.reshape(SIZES), AXES)
    placed = (
        P(AXES, None),
        P(AXES, None),
        P(AXES, None),
        P(AXES),
        P(AXES),
        P(AXES, None),
        P(("zh", "xa", "xb", "y"), None),
    )
    return jax.shard_map(
        body,
        mesh=fine,
        in_specs=placed,
        out_specs=(P(AXES, None), P(AXES), P(AXES, None), P(("zh", "xa", "xb", "y"))),
        check_vma=False,
    )
```
